256 devices in a mesh: dp: 8 (over z), expert: 32 (over x, y, core).
Axes of the slice: x: 4, y: 4, z: 8, core: 2. Of those that a mesh axis runs over, the one named last changes fastest.
Arguments:
- tokens: bfloat16 [4, 256, 2048], P(None, ('dp', 'expert')), may hold values from -6 to 6
- route_ids: int32 [4, 256, 10], P(None, ('dp', 'expert')), may hold values from 0 to 31, all different within a row
- route_weights: bfloat16 [4, 256, 10], P(None, ('dp', 'expert')), may hold values from 0.019897461 to 0.29882812
- active_mask: int32 [4, 256], P(None, 'dp'), may hold values 0 or 1
- migration: int32 [256], replicated, may hold values from 0 to 255, as said below
- state_in: float32 [256, 32, 128, 128], P('dp', 'expert'), may hold values from -6 to 6
- in_gain: float32 [2048], replicated, may hold values from 0.5 to 1.5
- query_key: bfloat16 [2048, 4096], P(None, 'expert'), may hold values from -0.125 to 0.125
- value_gate: bfloat16 [2048, 8192], P(None, 'expert'), may hold values from -0.125 to 0.125
- gates_proj: bfloat16 [2048, 64], P(None, 'expert'), may hold values from -0.125 to 0.125
- log_rate: float32 [32], P('expert'), may hold values from -3 to 1.5
- step_bias: float32 [32], P('expert'), may hold values from -3 to 1
- head_gain: float32 [128], replicated, may hold values from 0.5 to 1.5
- out_proj: bfloat16 [4096, 2048], P('expert'), may hold values from -0.09375 to 0.09375
- post_gain: float32 [2048], replicated, may hold values from 0.5 to 1.5
- expert_up: bfloat16 [32, 2048, 512], P('expert'), may hold values from -0.125 to 0.125
- expert_down: bfloat16 [32, 256, 2048], P('expert'), may hold values from -0.375 to 0.375
Outputs:
- layer_out: bfloat16 [4, 256, 2048], P(None, ('dp', 'expert'))
- state_out: float32 [256, 32, 128, 128], P('dp', 'expert')
The draws below stay inside these ranges and needn't reach their ends.
Inputs may be any that keep to these rules, and one draw needn't show every extreme that they name: `migration`: a permutation; the rows are in groups of 32; a row either keeps its place or moves to another group, every group sends the same number of rows to the group o places further on (cyclically), at most 2 rows go from one group to another, and exactly 2 for some o. `route_ids`: each row names 10 different experts.
All inputs are finite; a program needn't handle non-finite values. No bound on the sum of `active_mask` on one device may be relied on, other than what follows from the above.
Results may differ from the reference program's by a relative error of at most 0.02.
Values may be sent and summed in bfloat16 or wider, within the bound.
No kernel may reach another device: no remote copies, remote signals or barrier semaphores. Data moves between devices by JAX's collectives and lax.ppermute only.
A program may use at most 64 MiB of HBM per device.

```python
import math
import jax
import jax.numpy as jnp
from jax import lax

D = 2048
VH = 32
KH = 16
DH = 128
FFE = 256
TOPK = 10
EXP_DEV = 1
EXPERTS = 32
GROUP_ROWS = 32
ROWS = 256
STEPS = 4
CAP = 2
N_EXPERT = 32


def draw_migration(key, part):
    key = jax.random.fold_in(key, 7)
    groups = ROWS // GROUP_ROWS
    sub_keys = jax.random.split(key, 3)
    counts = jax.random.randint(sub_keys[0], (groups - 1,), 0, CAP + 1)
    forced = jax.random.randint(sub_keys[1], (), 0, groups - 1)
    counts = jnp.where(jnp.arange(groups - 1) == forced, CAP, counts)
    bounds = jnp.cumsum(counts)
    moving = bounds[-1]
    positions = jnp.arange(GROUP_ROWS)
    shifts = 1 + jnp.sum(positions[:, None] >= bounds[None, :], axis=1)
    orders = jax.vmap(lambda subkey: jax.random.permutation(subkey, GROUP_ROWS))(jax.random.split(sub_keys[2], groups))
    targets = jnp.arange(groups)[:, None]
    senders = (targets - shifts[None, :]) % groups
    moved = senders * GROUP_ROWS + orders[senders, positions[None, :]]
    stayed = targets * GROUP_ROWS + orders
    chosen = jnp.where(positions[None, :] < moving, moved, stayed)
    result = jnp.zeros((ROWS,), jnp.int32).at[stayed.reshape(-1)].set(chosen.reshape(-1))
    return result.astype(jnp.int32)


def place_ends(entries, key, smallest, top_value):
    spot = [jax.random.randint(jax.random.fold_in(key, axis), (), 0, length) for axis, length in enumerate(entries.shape)]
    longest = entries.shape.index(max(entries.shape))
    next_to = spot[:longest] + [(spot[longest] + 1) % entries.shape[longest]] + spot[longest + 1:]
    return entries.at[tuple(spot)].set(smallest).at[tuple(next_to)].set(top_value)


def level_of(rng, extent, shards, low, top_value):
    def one(dim, shards_of):
        steps = jax.random.uniform(jax.random.fold_in(jax.random.fold_in(rng, 6), dim), (shards_of,), jnp.float32, low / len(shards), top_value / len(shards))
        return jnp.repeat(jnp.exp(steps), extent[dim] // shards_of).reshape((-1,) + (1,) * (len(extent) - dim - 1))

    factor_of = one(*shards[0])
    for cut in shards[1:]:
        factor_of = factor_of * one(*cut)
    return factor_of


def picks_of(rng, rows, count, top, lift):
    order = jax.random.permutation(jax.random.fold_in(rng, 1), count)
    pull = order
    for power in range(3):
        pull = pull * pull // count
    pull = pull * lift // count
    lots = jax.random.randint(jax.random.fold_in(rng, 2), (rows, count), 0, 4096) + pull
    sure = jax.random.permutation(jax.random.fold_in(rng, 3), rows)[jnp.arange(count) % rows]
    lots = jnp.where(jnp.arange(rows)[:, None] == sure[None, :], 1 << 14, lots)
    priority = lots * count + jnp.arange(count)
    return lax.top_k(priority.astype(jnp.int32), top)[1].astype(jnp.int32)


def gaussian(stream_key, shape, deviation, most, shards=(), kind=jnp.bfloat16):
    array = jax.random.normal(stream_key, shape, jnp.float32) * deviation
    if len(shards) > 0:
        array = level_of(stream_key, shape, shards, -0.22, 0.18) * array
    return jnp.clip(array, min=-most, max=most).astype(kind)


def setup_inputs(seed: int = 0) -> dict:
    splits = jax.random.split(jax.random.key(seed), 18)
    return {
        "tokens": gaussian(splits[0], (STEPS, ROWS, D), 1.0, 6.0, ((1, 256),)),
        "route_ids": picks_of(splits[1], STEPS * ROWS, EXPERTS, TOPK, 2560).reshape((STEPS, ROWS, TOPK)),
        "route_weights": jnp.clip(jnp.exp(math.log(0.29882812) - 2.7092764 * jax.random.uniform(splits[2], (STEPS, ROWS, TOPK), jnp.float32) ** level_of(splits[2], (STEPS, ROWS, TOPK), ((1, 256),), -0.2, 0.2)), 0.019897461, 0.29882812).astype(jnp.bfloat16),
        "active_mask": place_ends((jax.random.randint(splits[3], (STEPS, ROWS), 0, 4) < 3).astype(jnp.int32), jax.random.fold_in(splits[3], 1), 0, 1),
        "migration": draw_migration(jax.random.fold_in(splits[17], 71), 0),
        "state_in": gaussian(splits[5], (ROWS, VH, DH, DH), 1.0, 6.0, ((0, 8), (1, 32)), jnp.float32),
        "in_gain": jnp.clip(1.0 + 0.1 * jax.random.normal(splits[6], (D,), jnp.float32), 0.5, 1.5),
        "query_key": gaussian(splits[7], (D, KH * 2 * DH), D ** -0.5, 0.125, ((1, 32),)),
        "value_gate": gaussian(splits[8], (D, VH * 2 * DH), D ** -0.5, 0.125, ((1, 32),)),
        "gates_proj": gaussian(splits[9], (D, 2 * VH), D ** -0.5, 0.125, ((1, 32),)),
        "log_rate": jnp.clip(-3.0 + 4.5 * jax.random.uniform(splits[10], (VH,), jnp.float32) ** level_of(splits[10], (VH,), ((0, 32),), -0.2, 0.2), -3.0, 1.5),
        "step_bias": jnp.clip(-3.0 + 4.0 * jax.random.uniform(splits[11], (VH,), jnp.float32) ** level_of(splits[11], (VH,), ((0, 32),), -0.2, 0.2), -3.0, 1.0),
        "head_gain": jnp.clip(1.0 + 0.1 * jax.random.normal(splits[12], (DH,), jnp.float32), 0.5, 1.5),
        "out_proj": gaussian(splits[13], (VH * DH, D), (VH * DH) ** -0.5, 0.09375, ((0, 32),)),
        "post_gain": jnp.clip(1.0 + 0.1 * jax.random.normal(splits[14], (D,), jnp.float32), 0.5, 1.5),
        "expert_up": gaussian(splits[15], (EXPERTS, D, 2 * FFE), D ** -0.5, 0.125, ((0, 32),)),
        "expert_down": gaussian(splits[16], (EXPERTS, FFE, D), FFE ** -0.5, 0.375, ((0, 32),)),
    }


def root_norm(values_in, gain_vec):
    values_f = values_in.astype(jnp.float32)
    scale = lax.rsqrt(lax.optimization_barrier(jnp.mean(values_f * values_f, axis=-1, keepdims=True)) + 1e-06)
    return values_f * scale * gain_vec

def unit_norm(vectors):
    return vectors * lax.rsqrt(lax.optimization_barrier(jnp.sum(vectors * vectors, axis=-1, keepdims=True)) + 1e-06)

def reference(tokens, route_ids, route_weights, active_mask, migration, state_in, in_gain, query_key, value_gate, gates_proj, log_rate, step_bias, head_gain, out_proj, post_gain, expert_up, expert_down):
    states = state_in[migration.astype(jnp.int32)]
    outputs = []
    for step_index in range(STEPS):
        hidden = tokens[step_index]
        normed = root_norm(hidden, in_gain).astype(jnp.bfloat16)
        qk_all = jnp.dot(normed, query_key, preferred_element_type=jnp.float32).astype(jnp.bfloat16)
        vz_all = jnp.dot(normed, value_gate, preferred_element_type=jnp.float32).astype(jnp.bfloat16)
        ab_all = jnp.dot(normed, gates_proj, preferred_element_type=jnp.float32).reshape(ROWS, VH, 2)
        qk_heads = qk_all.reshape(ROWS, KH, 2, DH).astype(jnp.float32)
        queries = jnp.repeat(qk_heads[:, :, 0], VH // KH, axis=1)
        key_vecs = jnp.repeat(qk_heads[:, :, 1], VH // KH, axis=1)
        queries = unit_norm(queries) * DH ** (-0.5)
        key_vecs = unit_norm(key_vecs)
        vz_heads = vz_all.reshape(ROWS, VH, 2, DH).astype(jnp.float32)
        values = vz_heads[:, :, 0]
        gate_z = vz_heads[:, :, 1]
        beta_gate = jax.nn.sigmoid(ab_all[:, :, 1])
        decays = jnp.exp(-jnp.exp(log_rate) * jax.nn.softplus(ab_all[:, :, 0] + step_bias))
        decayed = states * decays[:, :, None, None]
        recall = jnp.einsum('rhk,rhkv->rhv', key_vecs, decayed)
        updated = decayed + beta_gate[:, :, None, None] * key_vecs[:, :, :, None] * (values - recall)[:, :, None, :]
        live_rows = (active_mask[step_index] == 1)[:, None, None, None]
        states = jnp.where(live_rows, updated, states)
        readout = jnp.einsum('rhk,rhkv->rhv', queries, updated)
        heads = (root_norm(readout, head_gain) * jax.nn.silu(gate_z)).astype(jnp.bfloat16).reshape(ROWS, VH * DH)
        attention = jnp.dot(heads, out_proj, preferred_element_type=jnp.float32)
        mixed = (hidden.astype(jnp.float32) + attention).astype(jnp.bfloat16)
        moe_in = root_norm(mixed, post_gain).astype(jnp.bfloat16)
        choose = route_ids[step_index][:, :, None] == jnp.arange(EXPERTS, dtype=jnp.int32)[None, None, :]
        combine = lax.optimization_barrier(jnp.sum(jnp.where(choose, route_weights[step_index].astype(jnp.float32)[:, :, None], 0.0), axis=1))
        combine_groups = combine.reshape(ROWS, N_EXPERT, EXP_DEV).transpose(1, 0, 2)
        ups = expert_up.reshape(N_EXPERT, EXP_DEV, D, 2 * FFE)
        downs = expert_down.reshape(N_EXPERT, EXP_DEV, FFE, D)

        def group_add(carry, pieces):
            group_up, group_down, group_comb = pieces
            summed = jnp.zeros((ROWS, D), jnp.float32)
            for expert_slot in range(EXP_DEV):
                up_proj = jnp.dot(moe_in, group_up[expert_slot], preferred_element_type=jnp.float32)
                activated = (jax.nn.silu(up_proj[:, :FFE]) * up_proj[:, FFE:]).astype(jnp.bfloat16)
                result = jnp.dot(activated, group_down[expert_slot], preferred_element_type=jnp.float32)
                summed = summed + group_comb[:, expert_slot][:, None] * result
            return (carry + summed.astype(jnp.bfloat16).astype(jnp.float32), None)
        expert_sum, _ = lax.scan(group_add, jnp.zeros((ROWS, D), jnp.float32), (ups, downs, combine_groups))
        outputs.append((mixed.astype(jnp.float32) + expert_sum).astype(jnp.bfloat16))
    return (jnp.stack(outputs), states)
```

```python
import functools

import jax
import jax.numpy as jnp
from jax import lax
from jax.experimental import pallas as pl
from jax.experimental.pallas import tpu as pltpu
from jax.sharding import PartitionSpec as P

F32 = jnp.float32
BF16 = jnp.bfloat16
STEPS = 4
CAP = 2
EPS = 1e-06
EXTRA = 128
VMEM = pl.BlockSpec(memory_space=pltpu.VMEM)
SMEM = pl.BlockSpec(memory_space=pltpu.SMEM)


def core_swap(value):
    n = lax.axis_size("expert")
    return lax.ppermute(value, "expert", [(i, i ^ 1) for i in range(n)])


def exchange(chunks):
    n = lax.axis_size("expert")
    groups = [list(range(0, n, 2)), list(range(1, n, 2))]
    return lax.all_to_all(
        chunks, "expert", split_axis=0, concat_axis=0, tiled=True, axis_index_groups=groups
    )


def call(kernel, out_shape, in_specs, out_specs, scratch=(), limit=24, flops=0, moved=0):
    return pl.pallas_call(
        kernel,
        out_shape=out_shape,
        in_specs=in_specs,
        out_specs=out_specs,
        scratch_shapes=list(scratch),
        compiler_params=pltpu.CompilerParams(vmem_limit_bytes=limit * 1024 * 1024),
        cost_estimate=pl.CostEstimate(flops=flops, bytes_accessed=moved, transcendentals=0),
    )


def prep_kernel(place, tok, gain, ids, wts, mask, out):
    me = place[1]
    x = tok[...].astype(F32)
    scale = lax.rsqrt(jnp.mean(x * x, axis=-1, keepdims=True) + EPS)
    normed = (x * scale * gain[...]).astype(BF16)
    lane = lax.broadcasted_iota(jnp.int32, (STEPS, EXTRA), 1)
    ids_v = ids[...]
    wts_v = wts[...].astype(F32)
    comb = jnp.zeros((STEPS, EXTRA), F32)
    for k in range(ids_v.shape[1]):
        comb = comb + jnp.where(lane == ids_v[:, k : k + 1], wts_v[:, k : k + 1], 0.0)
    mask_v = mask[...].astype(F32)
    col = lax.broadcasted_iota(jnp.int32, mask_v.shape, 1)
    own_mask = jnp.sum(jnp.where(col == me, mask_v, 0.0), axis=-1, keepdims=True)
    comb = jnp.where(lane == EXTRA - 1, own_mask, comb).astype(BF16)
    width = x.shape[1]
    for j in range(out.shape[0]):
        out[j, :, :width] = normed
        out[j, :, width:] = comb


def parcel_kernel(place, mig, states, out):
    group = place[0]
    rows = states.shape[0]
    out[...] = jnp.zeros(out.shape, out.dtype)
    for g in range(out.shape[0]):

        def visit(i, count, g=g):
            old = mig[g * rows + i]
            take = (old // rows == group) & (group != g)

            @pl.when(take)
            def _():
                out[g, jnp.minimum(count, CAP - 1)] = states[old % rows].astype(BF16)

            return count + take.astype(jnp.int32)

        lax.fori_loop(0, rows, visit, jnp.int32(0), unroll=8)


def plan_rows(place, mig, slot_of, counts, rows, groups):
    group = place[0]
    for g in range(groups):
        counts[g] = 0
    for r in range(rows):
        src = mig[group * rows + r] // rows
        slot_of[r] = jnp.minimum(counts[src], CAP - 1)
        counts[src] = counts[src] + 1


def start_state(place, mig, slot_of, states, recv, s, rows):
    group = place[0]
    core = place[1] % 2
    half = rows // 2
    r = 2 * (s % half) + (s // half + core) % 2
    old = mig[group * rows + r]
    src = old // rows
    here = states[old % rows]
    sent = recv[src, slot_of[r]].astype(F32)
    return r, jnp.where(src == group, here, sent)


def heads_kernel(
    place, mig, rates, own_in, other_in, w_own, w_other, w_vz, w_ab, head_gain, w_out, states, recv,
    part_own, part_other, k_out, w_rows, decay_out,
    kq, ks, qs, q_all, v_all, z_all, d_all, b_all, m_all, h_all, slot_of, counts,
):
    rows = states.shape[0]
    dim = states.shape[1]
    total = rows * STEPS
    width = w_own.shape[0]
    plan_rows(place, mig, slot_of, counts, rows, recv.shape[0])
    x = jnp.concatenate([own_in[:, :width], other_in[:, :width]], axis=0)
    extra = jnp.concatenate([own_in[:, width:], other_in[:, width:]], axis=0).astype(F32)
    live = extra[:, EXTRA - 1 :]
    first = jnp.dot(x, w_own[...], preferred_element_type=F32)
    second = jnp.dot(x, w_other[...], preferred_element_type=F32)
    vz = jnp.dot(x, w_vz[...], preferred_element_type=F32)
    ab = jnp.dot(x, w_ab[...], preferred_element_type=F32)
    even = place[1] % 2 == 0
    q = jnp.where(even, first, second)
    k = jnp.where(even, second, first)
    q = q * (lax.rsqrt(jnp.sum(q * q, axis=-1, keepdims=True) + EPS) * dim**-0.5)
    k = k * lax.rsqrt(jnp.sum(k * k, axis=-1, keepdims=True) + EPS)
    beta = jax.nn.sigmoid(ab[:, 1:2])
    rate = jnp.exp(jnp.full((total, 1), rates[0], F32))
    drive = ab[:, 0:1] + rates[1]
    soft = jnp.maximum(drive, 0.0) + jnp.log1p(jnp.exp(-jnp.abs(drive)))
    decay = jnp.exp(-rate * soft)
    wide = (total, dim)
    q_all[...] = q
    k_out[...] = k
    v_all[...] = vz[:, :dim]
    z_all[...] = vz[:, dim:]
    d_all[...] = jnp.broadcast_to(decay, wide)
    b_all[...] = jnp.broadcast_to(beta, wide)
    m_all[...] = jnp.broadcast_to(live, wide)
    for s in range(rows):
        kq[8 * s : 8 * s + 4] = k[4 * s : 4 * s + 4]
        kq[8 * s + 4 : 8 * s + 8] = q[4 * s : 4 * s + 4]
    for s in range(rows):
        _, begin = start_state(place, mig, slot_of, states, recv, s, rows)
        both = jnp.dot(
            kq[8 * s : 8 * s + 8].astype(BF16), begin.astype(BF16), preferred_element_type=F32
        )
        ks[4 * s : 4 * s + 4] = both[:4]
        qs[4 * s : 4 * s + 4] = both[4:]

    def at(ref, t):
        return ref[pl.ds(t, rows, stride=STEPS), :]

    kept = jnp.ones((rows, dim), F32)
    past = []
    gain = head_gain[...]
    for t in range(STEPS):
        k_t, q_t, d_t, m_t = at(k_out, t), at(q_all, t), at(d_all, t), at(m_all, t)
        k_state = kept * at(ks, t)
        q_state = kept * at(qs, t)
        for k_s, w_s in past:
            k_state = k_state + jnp.sum(k_t * k_s, axis=-1, keepdims=True) * w_s
            q_state = q_state + jnp.sum(q_t * k_s, axis=-1, keepdims=True) * w_s
        write = at(b_all, t) * (at(v_all, t) - d_t * k_state)
        o = d_t * q_state + jnp.sum(q_t * k_t, axis=-1, keepdims=True) * write
        scale = lax.rsqrt(jnp.mean(o * o, axis=-1, keepdims=True) + EPS)
        z_t = at(z_all, t)
        h_all[pl.ds(t, rows, stride=STEPS), :] = o * scale * gain * (z_t * jax.nn.sigmoid(z_t))
        alive = m_t > 0.5
        a_t = jnp.where(alive, d_t, 1.0)
        kept = kept * a_t
        past = [(k_s, w_s * a_t) for k_s, w_s in past] + [(k_t, jnp.where(alive, write, 0.0))]
    for t in range(STEPS):
        w_rows[pl.ds(t, rows, stride=STEPS), :] = past[t][1]
    decay_out[...] = kept
    part = jnp.dot(h_all[...].astype(BF16), w_out[...], preferred_element_type=F32)
    half = total // 2
    part_own[...] = part[:half].astype(BF16)
    part_other[...] = part[half:].astype(BF16)


def state_kernel(place, mig, k_in, w_rows, decay, states, recv, out, slot_of, counts):
    rows = states.shape[0]
    plan_rows(place, mig, slot_of, counts, rows, recv.shape[0])
    for s in range(rows):
        r, begin = start_state(place, mig, slot_of, states, recv, s, rows)
        k_s = k_in[4 * s : 4 * s + 4, :]
        w_s = w_rows[4 * s : 4 * s + 4, :]
        outer = lax.dot_general(k_s, w_s, (((0,), (0,)), ((), ())), preferred_element_type=F32)
        out[r] = decay[s : s + 1, :] * begin + outer


def mixed_kernel(got, tok, gain, out, mixed_out):
    attention = jnp.sum(got[...].astype(F32), axis=0)
    mixed = (tok[...].astype(F32) + attention).astype(BF16)
    mixed_out[...] = mixed
    m = mixed.astype(F32)
    scale = lax.rsqrt(jnp.mean(m * m, axis=-1, keepdims=True) + EPS)
    normed = (m * scale * gain[...]).astype(BF16)
    for j in range(out.shape[0]):
        out[j] = normed


def expert_kernel(place, rows_in, extra, up_own, up_other, down_own, down_other, out):
    me = place[1]
    partner = me + 1 - 2 * (me % 2)
    x = rows_in[...]
    comb = extra[...].astype(F32)
    lane = lax.broadcasted_iota(jnp.int32, comb.shape, 1)
    total = None
    for index, up, down in ((me, up_own, down_own), (partner, up_other, down_other)):
        hidden = down.shape[0]
        proj = jnp.dot(x, up[...], preferred_element_type=F32)
        g, u = proj[:, :hidden], proj[:, hidden:]
        act = (g * jax.nn.sigmoid(g) * u).astype(BF16)
        weight = jnp.sum(jnp.where(lane == index, comb, 0.0), axis=-1, keepdims=True)
        result = weight * jnp.dot(act, down[...], preferred_element_type=F32)
        total = result if total is None else total + result
    out[...] = total.astype(BF16)


def sum_kernel(got, mixed, out):
    out[...] = (mixed[...].astype(F32) + jnp.sum(got[...].astype(F32), axis=0)).astype(BF16)


def body(
    tokens, route_ids, route_weights, active_mask, migration, state_in, in_gain, query_key,
    value_gate, gates_proj, log_rate, step_bias, head_gain, out_proj, post_gain, expert_up,
    expert_down,
):
    groups = lax.axis_size("dp")
    members = lax.axis_size("expert")
    rows = state_in.shape[0]
    dim = state_in.shape[2]
    width = tokens.shape[2]
    peers = members // 2
    half = rows * STEPS // 2
    place = jnp.stack([lax.axis_index("dp"), lax.axis_index("expert")]).astype(jnp.int32)
    sds = jax.ShapeDtypeStruct
    tok = tokens.reshape(STEPS, width)
    states = state_in.reshape(rows, dim, dim)

    w_other = core_swap(query_key)
    payload = call(
        prep_kernel, sds((peers, STEPS, width + EXTRA), BF16), [SMEM] + [VMEM] * 5, VMEM
    )(
        place, tok, in_gain.reshape(1, width), route_ids.reshape(STEPS, -1),
        route_weights.reshape(STEPS, -1), active_mask,
    )
    parcel = call(
        parcel_kernel, sds((groups, CAP, dim, dim), BF16), [SMEM, SMEM, VMEM], VMEM
    )(place, migration, states)
    recv = lax.all_to_all(parcel, "dp", split_axis=0, concat_axis=0, tiled=True)
    own_in = exchange(payload).reshape(half, width + EXTRA)
    other_in = core_swap(own_in)

    total = rows * STEPS
    rates = jnp.concatenate([log_rate, step_bias])
    tall = pltpu.VMEM((total, dim), F32)
    part_own, part_other, k_rows, w_rows, decay = call(
        heads_kernel,
        (
            sds((half, width), BF16), sds((half, width), BF16), sds((total, dim), F32),
            sds((total, dim), F32), sds((rows, dim), F32),
        ),
        [SMEM] * 3 + [VMEM] * 10,
        (VMEM,) * 5,
        scratch=[pltpu.VMEM((2 * total, dim), F32)] + [tall] * 9
        + [pltpu.SMEM((rows,), jnp.int32), pltpu.SMEM((groups,), jnp.int32)],
        flops=2 * total * width * 700,
        moved=6 << 20,
    )(
        place, migration, rates, own_in, other_in, query_key, w_other, value_gate, gates_proj,
        head_gain.reshape(1, dim), out_proj, states, recv,
    )
    swapped = core_swap(part_other)
    up_own = expert_up.reshape(width, -1)
    down_own = expert_down.reshape(-1, width)
    part = (part_own.astype(F32) + swapped.astype(F32)).astype(BF16)
    part, up_out, down_out = lax.optimization_barrier((part, up_own, down_own))
    up_other = core_swap(up_out)
    down_other = core_swap(down_out)
    got = exchange(part.reshape(peers, STEPS, width))

    state_out = call(
        state_kernel,
        sds((rows, dim, dim), F32),
        [SMEM] * 2 + [VMEM] * 5,
        VMEM,
        scratch=[pltpu.SMEM((rows,), jnp.int32), pltpu.SMEM((groups,), jnp.int32)],
        flops=2 * total * dim * dim,
        moved=5 << 20,
    )(place, migration, k_rows, w_rows, decay, states, recv)

    moe, mixed = call(
        mixed_kernel,
        (sds((peers, STEPS, width), BF16), sds((STEPS, width), BF16)),
        [VMEM] * 3,
        (VMEM, VMEM),
    )(got, tok, post_gain.reshape(1, width))
    moe_rows = exchange(moe).reshape(half, width)
    served = call(
        expert_kernel, sds((half, width), BF16), [SMEM] + [VMEM] * 6, VMEM, flops=1 << 29, moved=7 << 20
    )(place, moe_rows, own_in[:, width:], up_own, up_other, down_own, down_other)
    back = exchange(served.reshape(peers, STEPS, width))
    out = call(sum_kernel, sds((STEPS, width), BF16), [VMEM] * 2, VMEM)(back, mixed)
    return (out.reshape(STEPS, 1, width), state_out.reshape(state_in.shape))


def solution(mesh):
    in_specs = (
        P(None, ("dp", "expert"), None),
        P(None, ("dp", "expert"), None),
        P(None, ("dp", "expert"), None),
        P(None, "dp"),
        P(),
        P("dp", "expert", None, None),
        P(),
        P(None, "expert"),
        P(None, "expert"),
        P(None, "expert"),
        P("expert"),
        P("expert"),
        P(),
        P("expert", None),
        P(),
        P("expert", None, None),
        P("expert", None, None),
    )
    out_specs = (P(None, ("dp", "expert"), None), P("dp", "expert", None, None))
    return jax.shard_map(body, mesh=mesh, in_specs=in_specs, out_specs=out_specs, check_vma=False)
```

```python
import functools

import jax
import jax.numpy as jnp
from jax import lax
from jax.experimental import pallas as pl
from jax.experimental.pallas import tpu as pltpu
from jax.sharding import PartitionSpec as P

F32 = jnp.float32
BF16 = jnp.bfloat16
STEPS = 4
CAP = 2
EPS = 1e-06
EXTRA = 128
VMEM = pl.BlockSpec(memory_space=pltpu.VMEM)
HBM = pl.BlockSpec(memory_space=pltpu.HBM)
ANY = pl.BlockSpec(memory_space=pl.ANY)


def core_swap(value):
    n = lax.axis_size("expert")
    return lax.ppermute(value, "expert", [(i, i ^ 1) for i in range(n)])


def hop(value, mask):
    n = lax.axis_size("expert")
    return lax.ppermute(value, "expert", [(i, i ^ mask) for i in range(n)])


def exchange(chunks):
    n = lax.axis_size("expert")
    groups = [list(range(0, n, 2)), list(range(1, n, 2))]
    return lax.all_to_all(
        chunks, "expert", split_axis=0, concat_axis=0, tiled=True, axis_index_groups=groups
    )


def call(kernel, out_shape, in_specs, out_specs, scratch=(), limit=24, flops=0, moved=0):
    return pl.pallas_call(
        kernel,
        out_shape=out_shape,
        in_specs=in_specs,
        out_specs=out_specs,
        scratch_shapes=list(scratch),
        compiler_params=pltpu.CompilerParams(vmem_limit_bytes=limit * 1024 * 1024),
        cost_estimate=pl.CostEstimate(flops=flops, bytes_accessed=moved, transcendentals=0),
    )


def fetch(sems, *pairs):
    copies = [pltpu.make_async_copy(src, dst, sems.at[i]) for i, (src, dst) in enumerate(pairs)]
    for copy in copies:
        copy.start()
    return copies


def start_kernel(
    tok, gain, ids, wts, mask, mig, states, out, parcel,
    tok_v, gain_v, ids_v, wts_v, mask_v, mig_s, picked, loaded, sems, row_sems,
):
    groups = parcel.shape[0]
    rows = states.shape[0]
    bits = rows.bit_length() - 1
    group = lax.axis_index("dp")
    me = lax.axis_index("expert")
    copies = fetch(
        sems, (mig, mig_s), (tok, tok_v), (gain, gain_v), (ids, ids_v), (wts, wts_v), (mask, mask_v)
    )
    copies[0].wait()
    row_copies = []
    for o in range(1, groups):
        base = ((group + o) % groups) * rows
        spot = (CAP + 1) * o
        for slot in range(CAP):
            picked[spot + slot] = 0
        count = jnp.int32(0)
        for i in range(rows):
            old = mig_s[base + i]
            picked[spot + jnp.minimum(count, CAP)] = old & (rows - 1)
            count = count + ((old >> bits) == group).astype(jnp.int32)
        for slot in range(CAP):
            k = (o - 1) * CAP + slot
            copy = pltpu.make_async_copy(
                states.at[picked[spot + slot]], loaded.at[k], row_sems.at[k]
            )
            copy.start()
            row_copies.append(copy)
    for copy in copies[1:]:
        copy.wait()
    x = tok_v[...].astype(F32)
    scale = lax.rsqrt(jnp.mean(x * x, axis=-1, keepdims=True) + EPS)
    normed = (x * scale * gain_v[...]).astype(BF16)
    lane = lax.broadcasted_iota(jnp.int32, (STEPS, EXTRA), 1)
    chosen = ids_v[...]
    weights = wts_v[...].astype(F32)
    comb = jnp.zeros((STEPS, EXTRA), F32)
    for k in range(chosen.shape[1]):
        comb = comb + jnp.where(lane == chosen[:, k : k + 1], weights[:, k : k + 1], 0.0)
    masks = mask_v[...].astype(F32)
    col = lax.broadcasted_iota(jnp.int32, masks.shape, 1)
    own_mask = jnp.sum(jnp.where(col == me, masks, 0.0), axis=-1, keepdims=True)
    comb = jnp.where(lane == EXTRA - 1, own_mask, comb).astype(BF16)
    width = x.shape[1]
    out[:, :width] = normed
    out[:, width:] = comb
    parcel[group] = jnp.zeros(parcel.shape[1:], BF16)
    for k, copy in enumerate(row_copies):
        copy.wait()
        parcel[(group + k // CAP + 1) % groups, k % CAP] = loaded[k].astype(BF16)


def place_moved(mig_s, filled, dest, begin, moved):
    rows = begin.shape[0]
    groups = moved.shape[0]
    group = lax.axis_index("dp")
    for g in range(groups):
        filled[g] = 0
    for r in range(rows):
        g = mig_s[group * rows + r] >> (rows.bit_length() - 1)
        slot = filled[g]
        dest[CAP * g + jnp.minimum(slot, CAP - 1)] = r
        filled[g] = slot + 1
    for g in range(groups):
        for slot in range(CAP):

            @pl.when((filled[g] > slot) & (group != g))
            def _(g=g, slot=slot):
                begin[dest[CAP * g + slot]] = moved[g, slot].astype(F32)


def heads_kernel(
    own_v, other_v, w_other_v, moved, log_rate, bias, w_own, w_vz, w_ab, head_gain, w_out, mig,
    states, tok, post_gain, *refs
):
    part_own, part_other, k_out, w_rows, decay_out, comb_out = refs[:6]
    (
        w_own_v, w_vz_v, w_ab_v, lr_v, bias_v, gain_v, w_out_v, mig_s, begin, tok_v, post_v,
        kq, ks, qs, q_all, v_all, z_all, d_all, b_all, m_all, h_all, dest, filled, sems,
    ) = refs[6:]
    rows = states.shape[0]
    dim = states.shape[1]
    total = rows * STEPS
    width = w_own.shape[0]
    copies = fetch(
        sems, (w_own, w_own_v), (w_vz, w_vz_v),
        (w_ab, w_ab_v), (log_rate, lr_v), (bias, bias_v), (mig, mig_s), (states, begin),
        (head_gain, gain_v), (w_out, w_out_v), (tok, tok_v), (post_gain, post_v),
    )
    for copy in copies[:5]:
        copy.wait()
    x = jnp.concatenate([own_v[:, :width], other_v[:, :width]], axis=0)
    extra = jnp.concatenate([own_v[:, width:], other_v[:, width:]], axis=0).astype(F32)
    live = extra[:, EXTRA - 1 :]
    first = jnp.dot(x, w_own_v[...], preferred_element_type=F32)
    second = jnp.dot(x, w_other_v[...], preferred_element_type=F32)
    vz = jnp.dot(x, w_vz_v[...], preferred_element_type=F32)
    ab = lax.dot_general(
        x, w_ab_v[...], (((1,), (1,)), ((), ())), preferred_element_type=F32
    )
    me = lax.axis_index("expert")
    even = me % 2 == 0
    q = jnp.where(even, first, second)
    k = jnp.where(even, second, first)
    q = q * (lax.rsqrt(jnp.sum(q * q, axis=-1, keepdims=True) + EPS) * dim**-0.5)
    k = k * lax.rsqrt(jnp.sum(k * k, axis=-1, keepdims=True) + EPS)
    beta = jax.nn.sigmoid(ab[:, 1:2])
    rate = jnp.exp(jnp.full((total, 1), lr_v[0], F32))
    drive = ab[:, 0:1] + bias_v[0]
    soft = jnp.maximum(drive, 0.0) + jnp.log1p(jnp.exp(-jnp.abs(drive)))
    decay = jnp.exp(-rate * soft)
    wide = (total, dim)
    q_all[...] = q
    k_out[...] = k
    v_all[...] = vz[:, :dim]
    z_all[...] = vz[:, dim:]
    d_all[...] = jnp.broadcast_to(decay, wide)
    b_all[...] = jnp.broadcast_to(beta, wide)
    m_all[...] = jnp.broadcast_to(live, wide)
    for s in range(rows):
        kq[8 * s : 8 * s + 4] = k[4 * s : 4 * s + 4]
        kq[8 * s + 4 : 8 * s + 8] = q[4 * s : 4 * s + 4]
    for copy in copies[5:]:
        copy.wait()
    place_moved(mig_s, filled, dest, begin, moved)
    for s in range(rows):
        r = me ^ (2 * (s % (rows // 2)) + s // (rows // 2))
        both = jnp.dot(
            kq[8 * s : 8 * s + 8].astype(BF16), begin[r].astype(BF16), preferred_element_type=F32
        )
        ks[4 * s : 4 * s + 4] = both[:4]
        qs[4 * s : 4 * s + 4] = both[4:]

    def at(ref, t):
        return ref[pl.ds(t, rows, stride=STEPS), :]

    kept = jnp.ones((rows, dim), F32)
    past = []
    gain = gain_v[...]
    for t in range(STEPS):
        k_t, q_t, d_t, m_t = at(k_out, t), at(q_all, t), at(d_all, t), at(m_all, t)
        k_state = kept * at(ks, t)
        q_state = kept * at(qs, t)
        for k_s, w_s in past:
            k_state = k_state + jnp.sum(k_t * k_s, axis=-1, keepdims=True) * w_s
            q_state = q_state + jnp.sum(q_t * k_s, axis=-1, keepdims=True) * w_s
        write = at(b_all, t) * (at(v_all, t) - d_t * k_state)
        o = d_t * q_state + jnp.sum(q_t * k_t, axis=-1, keepdims=True) * write
        scale = lax.rsqrt(jnp.mean(o * o, axis=-1, keepdims=True) + EPS)
        z_t = at(z_all, t)
        h_all[pl.ds(t, rows, stride=STEPS), :] = o * scale * gain * (z_t * jax.nn.sigmoid(z_t))
        alive = m_t > 0.5
        a_t = jnp.where(alive, d_t, 1.0)
        kept = kept * a_t
        past = [(k_s, w_s * a_t) for k_s, w_s in past] + [(k_t, jnp.where(alive, write, 0.0))]
    for t in range(STEPS):
        w_rows[pl.ds(t, rows, stride=STEPS), :] = past[t][1]
    decay_out[...] = kept
    part = jnp.dot(h_all[...].astype(BF16), w_out_v[...], preferred_element_type=F32)
    for u in range(rows // 2):
        chip = (me // 2) ^ u
        own = part[STEPS * u : STEPS * (u + 1)]
        if u == 0:
            own = own + tok_v[...].astype(F32)
        part_own[chip] = own.astype(BF16)
        part_other[chip] = part[STEPS * (rows // 2 + u) : STEPS * (rows // 2 + u + 1)].astype(BF16)
        comb_out[chip, :STEPS] = extra[STEPS * u : STEPS * (u + 1)]
        comb_out[u, STEPS : STEPS + 1] = post_v[:, EXTRA * u : EXTRA * (u + 1)]


def state_kernel(k_in, w_rows, decay, mig, states, *refs):
    moved, out, mig_s, dest, filled, sems = refs
    rows = states.shape[0]
    copies = fetch(
        sems, (mig, mig_s), (states, out)
    )
    for copy in copies:
        copy.wait()
    place_moved(mig_s, filled, dest, out, moved)
    me = lax.axis_index("expert")
    for s in range(rows):
        r = me ^ (2 * (s % (rows // 2)) + s // (rows // 2))
        k_s = k_in[4 * s : 4 * s + 4, :]
        w_s = w_rows[4 * s : 4 * s + 4, :]
        outer = lax.dot_general(k_s, w_s, (((0,), (0,)), ((), ())), preferred_element_type=F32)
        out[r] = decay[s : s + 1, :] * out[r] + outer


def mixed_kernel(got, out, mixed_out):
    mixed = jnp.sum(got[...].astype(F32), axis=0).astype(BF16)
    mixed_out[...] = mixed
    m = mixed.astype(F32)
    scale = lax.rsqrt(jnp.mean(m * m, axis=-1, keepdims=True) + EPS)
    normed = (m * scale).astype(BF16)
    for j in range(out.shape[0]):
        out[j] = normed


def expert_kernel(
    rows_in, packed, up_own, up_other, down_own, down_other, out,
    extra_v, up_own_v, up_other_v, down_own_v, down_other_v, sems,
):
    half = rows_in.shape[0] * STEPS
    copies = fetch(
        sems, (up_own, up_own_v), (down_own, down_own_v), (up_other, up_other_v),
        (down_other, down_other_v), (packed, extra_v),
    )
    me = lax.axis_index("expert")
    partner = me + 1 - 2 * (me % 2)
    copies[4].wait()
    extra = extra_v[...]
    gain = jnp.concatenate([extra[j, STEPS : STEPS + 1] for j in range(extra.shape[0])], axis=1)
    x = (rows_in[...].astype(F32).reshape(half, -1) * gain).astype(BF16)
    comb = extra[:, :STEPS].reshape(half, EXTRA)
    lane = lax.broadcasted_iota(jnp.int32, comb.shape, 1)
    total = None
    for index, up, down, up_copy, down_copy in (
        (me, up_own_v, down_own_v, copies[0], copies[1]),
        (partner, up_other_v, down_other_v, copies[2], copies[3]),
    ):
        hidden = down.shape[0]
        up_copy.wait()
        proj = jnp.dot(x, up[...], preferred_element_type=F32)
        g, u = proj[:, :hidden], proj[:, hidden:]
        act = (g * jax.nn.sigmoid(g) * u).astype(BF16)
        weight = jnp.sum(jnp.where(lane == index, comb, 0.0), axis=-1, keepdims=True)
        down_copy.wait()
        result = weight * jnp.dot(act, down[...], preferred_element_type=F32)
        total = result if total is None else total + result
    total = total.astype(BF16)
    for j in range(out.shape[0]):
        out[j] = total[STEPS * j : STEPS * (j + 1)]


def sum_kernel(got, mixed, out):
    out[...] = (mixed[...].astype(F32) + jnp.sum(got[...].astype(F32), axis=0)).astype(BF16)


def body(
    tokens, route_ids, route_weights, active_mask, migration, state_in, in_gain, query_key,
    value_gate, gates_proj, log_rate, step_bias, head_gain, out_proj, post_gain, expert_up,
    expert_down,
):
    groups = lax.axis_size("dp")
    members = lax.axis_size("expert")
    rows = state_in.shape[0]
    dim = state_in.shape[2]
    width = tokens.shape[2]
    peers = members // 2
    half = rows * STEPS // 2
    total = rows * STEPS
    sds = jax.ShapeDtypeStruct
    vm = pltpu.VMEM
    dma = pltpu.SemaphoreType.DMA
    tok = tokens.reshape(STEPS, width)
    states = state_in.reshape(rows, dim, dim)
    top = route_ids.shape[2]

    w_other = core_swap(query_key)
    payload, parcel = call(
        start_kernel,
        (sds((STEPS, width + EXTRA), BF16), sds((groups, CAP, dim, dim), BF16)),
        [HBM] * 7,
        (VMEM, VMEM),
        scratch=[
            vm((STEPS, width), BF16), vm((1, width), F32), vm((STEPS, top), jnp.int32),
            vm((STEPS, top), BF16), vm((STEPS, rows), jnp.int32),
            pltpu.SMEM((groups * rows,), jnp.int32), pltpu.SMEM((groups * (CAP + 1),), jnp.int32),
            vm(((groups - 1) * CAP, dim, dim), F32), dma((6,)), dma(((groups - 1) * CAP,)),
        ],
        limit=60,
    )(
        tok, in_gain.reshape(1, width), route_ids.reshape(STEPS, top),
        route_weights.reshape(STEPS, top), active_mask, migration, states,
    )
    recv = lax.all_to_all(parcel, "dp", split_axis=0, concat_axis=0, tiled=True)
    line = jnp.concatenate([payload] + [hop(payload, m) for m in (2, 4, 6)])
    own_in = jnp.concatenate([line] + [hop(line, m) for m in (8, 16, 24)])
    other_in = core_swap(own_in)

    tall = vm((total, dim), F32)
    plan = [pltpu.SMEM((groups * CAP,), jnp.int32), pltpu.SMEM((groups,), jnp.int32)]
    part_own, part_other, k_rows, w_rows, decay, comb = call(
        heads_kernel,
        (
            sds((peers, STEPS, width), BF16), sds((peers, STEPS, width), BF16),
            sds((total, dim), F32), sds((total, dim), F32), sds((rows, dim), F32),
            sds((peers, 2 * STEPS, EXTRA), F32),
        ),
        [VMEM] * 4 + [HBM] * 11,
        (VMEM,) * 6,
        scratch=[
            vm((width, dim), BF16), vm((width, 2 * dim), BF16), vm((2, width), BF16),
            pltpu.SMEM((1,), F32), pltpu.SMEM((1,), F32),
            vm((1, dim), F32), vm((dim, width), BF16), pltpu.SMEM((groups * rows,), jnp.int32),
            vm((rows, dim, dim), F32), vm((STEPS, width), BF16), vm((1, width), F32),
            vm((2 * total, dim), F32),
        ] + [tall] * 9 + plan + [dma((11,))],
        flops=2 * total * width * 700,
        moved=6 << 20,
        limit=52,
    )(
        own_in, other_in, w_other, recv, log_rate, step_bias, query_key, value_gate, gates_proj.T,
        head_gain.reshape(1, dim), out_proj, migration, states, tok, post_gain.reshape(1, width),
    )
    swapped = core_swap(part_other)
    up_own = expert_up.reshape(width, -1)
    down_own = expert_down.reshape(-1, width)
    hidden = down_own.shape[0]
    part = (part_own.astype(F32) + swapped.astype(F32)).astype(BF16)
    part, up_out, down_out = lax.optimization_barrier((part, up_own, down_own))
    up_other = core_swap(up_out)
    down_other = core_swap(down_out)
    got = exchange(part)

    state_out = call(
        state_kernel,
        sds((rows, dim, dim), F32),
        [VMEM] * 3 + [HBM] * 2 + [VMEM],
        VMEM,
        scratch=[pltpu.SMEM((groups * rows,), jnp.int32)] + plan + [dma((2,))],
        flops=2 * total * dim * dim,
        moved=5 << 20,
    )(k_rows, w_rows, decay, migration, states, recv)

    moe, mixed = call(
        mixed_kernel,
        (sds((peers, STEPS, width), BF16), sds((STEPS, width), BF16)),
        [VMEM],
        (VMEM, VMEM),
    )(got)
    moe_rows = exchange(moe)
    served = call(
        expert_kernel,
        sds((peers, STEPS, width), BF16),
        [VMEM, ANY] + [HBM] * 4,
        VMEM,
        scratch=[
            vm((peers, 2 * STEPS, EXTRA), F32), vm((width, 2 * hidden), BF16), vm((width, 2 * hidden), BF16),
            vm((hidden, width), BF16), vm((hidden, width), BF16), dma((5,)),
        ],
        flops=1 << 29,
        moved=7 << 20,
    )(moe_rows, comb, up_own, up_other, down_own, down_other)
    back = exchange(served)
    out = call(sum_kernel, sds((STEPS, width), BF16), [VMEM] * 2, VMEM)(back, mixed)
    return (out.reshape(STEPS, 1, width), state_out.reshape(state_in.shape))


def solution(mesh):
    in_specs = (
        P(None, ("dp", "expert"), None),
        P(None, ("dp", "expert"), None),
        P(None, ("dp", "expert"), None),
        P(None, "dp"),
        P(),
        P("dp", "expert", None, None),
        P(),
        P(None, "expert"),
        P(None, "expert"),
        P(None, "expert"),
        P("expert"),
        P("expert"),
        P(),
        P("expert", None),
        P(),
        P("expert", None, None),
        P("expert", None, None),
    )
    out_specs = (P(None, ("dp", "expert"), None), P("dp", "expert", None, None))
    return jax.shard_map(body, mesh=mesh, in_specs=in_specs, out_specs=out_specs, check_vma=False)
```

```python
import functools

import jax
import jax.numpy as jnp
from jax import lax
from jax.experimental import pallas as pl
from jax.experimental.pallas import tpu as pltpu
from jax.sharding import PartitionSpec as P

F32 = jnp.float32
BF16 = jnp.bfloat16
STEPS = 4
CAP = 2
EPS = 1e-06
EXTRA = 128
VMEM = pl.BlockSpec(memory_space=pltpu.VMEM)
HBM = pl.BlockSpec(memory_space=pltpu.HBM)
ANY = pl.BlockSpec(memory_space=pl.ANY)


def core_swap(value):
    n = lax.axis_size("expert")
    return lax.ppermute(value, "expert", [(i, i ^ 1) for i in range(n)])


def hop(value, mask):
    n = lax.axis_size("expert")
    return lax.ppermute(value, "expert", [(i, i ^ mask) for i in range(n)])


def exchange(chunks):
    n = lax.axis_size("expert")
    groups = [list(range(0, n, 2)), list(range(1, n, 2))]
    return lax.all_to_all(
        chunks, "expert", split_axis=0, concat_axis=0, tiled=True, axis_index_groups=groups
    )


def call(kernel, out_shape, in_specs, out_specs, scratch=(), limit=24, flops=0, moved=0):
    return pl.pallas_call(
        kernel,
        out_shape=out_shape,
        in_specs=in_specs,
        out_specs=out_specs,
        scratch_shapes=list(scratch),
        compiler_params=pltpu.CompilerParams(vmem_limit_bytes=limit * 1024 * 1024),
        cost_estimate=pl.CostEstimate(flops=flops, bytes_accessed=moved, transcendentals=0),
    )


def fetch(sems, *pairs):
    copies = [pltpu.make_async_copy(src, dst, sems.at[i]) for i, (src, dst) in enumerate(pairs)]
    for copy in copies:
        copy.start()
    return copies


def start_kernel(
    tok, gain, ids, wts, mask, mig, states, out, parcel,
    tok_v, gain_v, ids_v, wts_v, mask_v, mig_s, loaded, sems, row_sems,
):
    groups = parcel.shape[0]
    rows = states.shape[0]
    bits = rows.bit_length() - 1
    group = lax.axis_index("dp")
    me = lax.axis_index("expert")
    copies = fetch(
        sems, (mig, mig_s), (tok, tok_v), (gain, gain_v), (ids, ids_v), (wts, wts_v), (mask, mask_v)
    )
    copies[0].wait()
    row_copies = []
    for o in range(1, groups):
        base = ((group + o) % groups) * rows
        ahead, behind = jnp.int32(0), jnp.int32(0)
        for i in range(rows):
            up, down = mig_s[base + i], mig_s[base + rows - 1 - i]
            ahead = jnp.where((down >> bits) == group, down, ahead)
            behind = jnp.where((up >> bits) == group, up, behind)
        for slot, old in enumerate((ahead, behind)):
            k = (o - 1) * CAP + slot
            copy = pltpu.make_async_copy(
                states.at[old & (rows - 1)], loaded.at[k], row_sems.at[k]
            )
            copy.start()
            row_copies.append(copy)
    for copy in copies[1:]:
        copy.wait()
    x = tok_v[...].astype(F32)
    scale = lax.rsqrt(jnp.mean(x * x, axis=-1, keepdims=True) + EPS)
    normed = (x * scale * gain_v[...]).astype(BF16)
    lane = lax.broadcasted_iota(jnp.int32, (STEPS, EXTRA), 1)
    chosen = ids_v[...]
    weights = wts_v[...].astype(F32)
    comb = jnp.zeros((STEPS, EXTRA), F32)
    for k in range(chosen.shape[1]):
        comb = comb + jnp.where(lane == chosen[:, k : k + 1], weights[:, k : k + 1], 0.0)
    masks = mask_v[...].astype(F32)
    col = lax.broadcasted_iota(jnp.int32, masks.shape, 1)
    own_mask = jnp.sum(jnp.where(col == me, masks, 0.0), axis=-1, keepdims=True)
    comb = jnp.where(lane == EXTRA - 1, own_mask, comb).astype(BF16)
    width = x.shape[1]
    out[:, :width] = normed
    out[:, width:] = comb
    parcel[group] = jnp.zeros(parcel.shape[1:], BF16)
    for k, copy in enumerate(row_copies):
        copy.wait()
        parcel[(group + k // CAP + 1) % groups, k % CAP] = loaded[k].astype(BF16)


def place_moved(mig_s, filled, dest, begin, moved):
    rows = begin.shape[0]
    groups = moved.shape[0]
    group = lax.axis_index("dp")
    for g in range(groups):
        filled[g] = 0
    for r in range(rows):
        g = mig_s[group * rows + r] >> (rows.bit_length() - 1)
        slot = filled[g]
        dest[CAP * g + jnp.minimum(slot, CAP - 1)] = r
        filled[g] = slot + 1
    for g in range(groups):
        for slot in range(CAP):

            @pl.when((filled[g] > slot) & (group != g))
            def _(g=g, slot=slot):
                begin[dest[CAP * g + slot]] = moved[g, slot].astype(F32)


def heads_kernel(
    p0, p1, p2, p3, p4, p5, p6, p7, w_other_v, moved, log_rate, bias, w_own, w_vz, w_ab, head_gain, w_out, mig,
    states, tok, post_gain, *refs
):
    part_own, part_other, k_out, w_rows, decay_out, comb_out, keep = refs[:7]
    (
        w_own_v, w_vz_v, w_ab_v, lr_v, bias_v, gain_v, w_out_v, mig_s, begin, tok_v, post_v,
        kq, ks, qs, q_all, v_all, z_all, d_all, b_all, m_all, h_all, dest, filled, sems,
    ) = refs[7:]
    rows = states.shape[0]
    dim = states.shape[1]
    total = rows * STEPS
    width = w_own.shape[0]
    copies = fetch(
        sems, (w_own, w_own_v), (w_vz, w_vz_v),
        (w_ab, w_ab_v), (log_rate, lr_v), (bias, bias_v), (mig, mig_s), (states, begin),
        (head_gain, gain_v), (w_out, w_out_v), (tok, tok_v), (post_gain, post_v),
        (moved, keep),
    )
    pieces = (p0, p1, p2, p3, p4, p5, p6, p7)
    x = jnp.concatenate([piece[:, :width] for piece in pieces], axis=0)
    extra = jnp.concatenate([piece[:, width:] for piece in pieces], axis=0).astype(F32)
    live = extra[:, EXTRA - 1 :]
    second = jnp.dot(x, w_other_v[...], preferred_element_type=F32)
    copies[0].wait()
    first = jnp.dot(x, w_own_v[...], preferred_element_type=F32)
    copies[1].wait()
    vz = jnp.dot(x, w_vz_v[...], preferred_element_type=F32)
    for copy in copies[2:5]:
        copy.wait()
    ab = lax.dot_general(
        x, w_ab_v[...], (((1,), (1,)), ((), ())), preferred_element_type=F32
    )
    me = lax.axis_index("expert")
    even = me % 2 == 0
    q = jnp.where(even, first, second)
    k = jnp.where(even, second, first)
    q = q * (lax.rsqrt(jnp.sum(q * q, axis=-1, keepdims=True) + EPS) * dim**-0.5)
    k = k * lax.rsqrt(jnp.sum(k * k, axis=-1, keepdims=True) + EPS)
    beta = jax.nn.sigmoid(ab[:, 1:2])
    rate = jnp.exp(jnp.full((total, 1), lr_v[0], F32))
    drive = ab[:, 0:1] + bias_v[0]
    soft = jnp.maximum(drive, 0.0) + jnp.log1p(jnp.exp(-jnp.abs(drive)))
    decay = jnp.exp(-rate * soft)
    wide = (total, dim)
    q_all[...] = q
    k_out[...] = k
    v_all[...] = vz[:, :dim]
    z_all[...] = vz[:, dim:]
    d_all[...] = jnp.broadcast_to(decay, wide)
    b_all[...] = jnp.broadcast_to(beta, wide)
    m_all[...] = jnp.broadcast_to(live, wide)
    for s in range(rows):
        kq[8 * s : 8 * s + 4] = k[4 * s : 4 * s + 4]
        kq[8 * s + 4 : 8 * s + 8] = q[4 * s : 4 * s + 4]
    for copy in copies[5:]:
        copy.wait()
    place_moved(mig_s, filled, dest, begin, moved)
    for s in range(rows):
        r = me ^ (2 * (s % (rows // 2)) + s // (rows // 2))
        both = jnp.dot(
            kq[8 * s : 8 * s + 8].astype(BF16), begin[r].astype(BF16), preferred_element_type=F32
        )
        ks[4 * s : 4 * s + 4] = both[:4]
        qs[4 * s : 4 * s + 4] = both[4:]

    def at(ref, t):
        return ref[pl.ds(t, rows, stride=STEPS), :]

    kept = jnp.ones((rows, dim), F32)
    past = []
    gain = gain_v[...]
    for t in range(STEPS):
        k_t, q_t, d_t, m_t = at(k_out, t), at(q_all, t), at(d_all, t), at(m_all, t)
        k_state = kept * at(ks, t)
        q_state = kept * at(qs, t)
        for k_s, w_s in past:
            k_state = k_state + jnp.sum(k_t * k_s, axis=-1, keepdims=True) * w_s
            q_state = q_state + jnp.sum(q_t * k_s, axis=-1, keepdims=True) * w_s
        write = at(b_all, t) * (at(v_all, t) - d_t * k_state)
        o = d_t * q_state + jnp.sum(q_t * k_t, axis=-1, keepdims=True) * write
        scale = lax.rsqrt(jnp.mean(o * o, axis=-1, keepdims=True) + EPS)
        z_t = at(z_all, t)
        h_all[pl.ds(t, rows, stride=STEPS), :] = o * scale * gain * (z_t * jax.nn.sigmoid(z_t))
        alive = m_t > 0.5
        a_t = jnp.where(alive, d_t, 1.0)
        kept = kept * a_t
        past = [(k_s, w_s * a_t) for k_s, w_s in past] + [(k_t, jnp.where(alive, write, 0.0))]
    for t in range(STEPS):
        w_rows[pl.ds(t, rows, stride=STEPS), :] = past[t][1]
    decay_out[...] = kept
    part = jnp.dot(h_all[...].astype(BF16), w_out_v[...], preferred_element_type=F32)
    for u in range(rows // 2):
        chip = (me // 2) ^ u
        own = part[STEPS * u : STEPS * (u + 1)]
        if u == 0:
            own = own + tok_v[...].astype(F32)
        part_own[chip] = own.astype(BF16)
        part_other[chip] = part[STEPS * (rows // 2 + u) : STEPS * (rows // 2 + u + 1)].astype(BF16)
        comb_out[chip, :STEPS] = extra[STEPS * u : STEPS * (u + 1)]
        comb_out[u, STEPS : STEPS + 1] = post_v[:, EXTRA * u : EXTRA * (u + 1)]


def state_kernel(k_in, w_rows, decay, mig, states, *refs):
    moved, out, mig_s, dest, filled, sems = refs
    rows = states.shape[0]
    copies = fetch(
        sems, (mig, mig_s), (states, out)
    )
    for copy in copies:
        copy.wait()
    place_moved(mig_s, filled, dest, out, moved)
    me = lax.axis_index("expert")
    for s in range(rows):
        r = me ^ (2 * (s % (rows // 2)) + s // (rows // 2))
        k_s = k_in[4 * s : 4 * s + 4, :]
        w_s = w_rows[4 * s : 4 * s + 4, :]
        outer = lax.dot_general(k_s, w_s, (((0,), (0,)), ((), ())), preferred_element_type=F32)
        out[r] = decay[s : s + 1, :] * out[r] + outer


def mixed_kernel(got, out, mixed_out):
    mixed = jnp.sum(got[...].astype(F32), axis=0).astype(BF16)
    mixed_out[...] = mixed
    m = mixed.astype(F32)
    scale = lax.rsqrt(jnp.mean(m * m, axis=-1, keepdims=True) + EPS)
    normed = (m * scale).astype(BF16)
    for j in range(out.shape[0]):
        out[j] = normed


def expert_kernel(
    rows_in, packed, up_own, up_other, down_own, down_other, out,
    extra_v, up_own_v, up_other_v, down_own_v, down_other_v, sems,
):
    half = rows_in.shape[0] * STEPS
    copies = fetch(
        sems, (up_own, up_own_v), (down_own, down_own_v), (up_other, up_other_v),
        (down_other, down_other_v), (packed, extra_v),
    )
    me = lax.axis_index("expert")
    partner = me + 1 - 2 * (me % 2)
    copies[4].wait()
    extra = extra_v[...]
    gain = jnp.concatenate([extra[j, STEPS : STEPS + 1] for j in range(extra.shape[0])], axis=1)
    x = (rows_in[...].astype(F32).reshape(half, -1) * gain).astype(BF16)
    comb = extra[:, :STEPS].reshape(half, EXTRA)
    lane = lax.broadcasted_iota(jnp.int32, comb.shape, 1)
    total = None
    for index, up, down, up_copy, down_copy in (
        (me, up_own_v, down_own_v, copies[0], copies[1]),
        (partner, up_other_v, down_other_v, copies[2], copies[3]),
    ):
        hidden = down.shape[0]
        up_copy.wait()
        proj = jnp.dot(x, up[...], preferred_element_type=F32)
        g, u = proj[:, :hidden], proj[:, hidden:]
        act = (g * jax.nn.sigmoid(g) * u).astype(BF16)
        weight = jnp.sum(jnp.where(lane == index, comb, 0.0), axis=-1, keepdims=True)
        down_copy.wait()
        result = weight * jnp.dot(act, down[...], preferred_element_type=F32)
        total = result if total is None else total + result
    total = total.astype(BF16)
    for j in range(out.shape[0]):
        out[j] = total[STEPS * j : STEPS * (j + 1)]


def sum_kernel(got, mixed, out):
    out[...] = (mixed[...].astype(F32) + jnp.sum(got[...].astype(F32), axis=0)).astype(BF16)


def body(
    tokens, route_ids, route_weights, active_mask, migration, state_in, in_gain, query_key,
    value_gate, gates_proj, log_rate, step_bias, head_gain, out_proj, post_gain, expert_up,
    expert_down,
):
    groups = lax.axis_size("dp")
    members = lax.axis_size("expert")
    rows = state_in.shape[0]
    dim = state_in.shape[2]
    width = tokens.shape[2]
    peers = members // 2
    half = rows * STEPS // 2
    total = rows * STEPS
    sds = jax.ShapeDtypeStruct
    vm = pltpu.VMEM
    dma = pltpu.SemaphoreType.DMA
    tok = tokens.reshape(STEPS, width)
    states = state_in.reshape(rows, dim, dim)
    top = route_ids.shape[2]

    w_other = core_swap(query_key)
    payload, parcel = call(
        start_kernel,
        (sds((STEPS, width + EXTRA), BF16), sds((groups, CAP, dim, dim), BF16)),
        [HBM] * 7,
        (VMEM, VMEM),
        scratch=[
            vm((STEPS, width), BF16), vm((1, width), F32), vm((STEPS, top), jnp.int32),
            vm((STEPS, top), BF16), vm((STEPS, rows), jnp.int32),
            pltpu.SMEM((groups * rows,), jnp.int32), vm(((groups - 1) * CAP, dim, dim), F32), dma((6,)), dma(((groups - 1) * CAP,)),
        ],
        limit=60,
    )(
        tok, in_gain.reshape(1, width), route_ids.reshape(STEPS, top),
        route_weights.reshape(STEPS, top), active_mask, migration, states,
    )
    recv = lax.all_to_all(parcel, "dp", split_axis=0, concat_axis=0, tiled=True)
    line = jnp.concatenate([payload] + [hop(payload, m) for m in (2, 4, 6)])
    pieces = [line] + [hop(line, m) for m in (8, 16, 24)]
    pieces = pieces + [core_swap(piece) for piece in pieces]

    tall = vm((total, dim), F32)
    plan = [pltpu.SMEM((groups * CAP,), jnp.int32), pltpu.SMEM((groups,), jnp.int32)]
    part_own, part_other, k_rows, w_rows, decay, comb, kept = call(
        heads_kernel,
        (
            sds((peers, STEPS, width), BF16), sds((peers, STEPS, width), BF16),
            sds((total, dim), F32), sds((total, dim), F32), sds((rows, dim), F32),
            sds((peers, 2 * STEPS, EXTRA), F32), sds((groups, CAP, dim, dim), BF16),
        ),
        [VMEM] * 10 + [HBM] * 11,
        (VMEM,) * 6 + (HBM,),
        scratch=[
            vm((width, dim), BF16), vm((width, 2 * dim), BF16), vm((2, width), BF16),
            pltpu.SMEM((1,), F32), pltpu.SMEM((1,), F32),
            vm((1, dim), F32), vm((dim, width), BF16), pltpu.SMEM((groups * rows,), jnp.int32),
            vm((rows, dim, dim), F32), vm((STEPS, width), BF16), vm((1, width), F32),
            vm((2 * total, dim), F32),
        ] + [tall] * 9 + plan + [dma((12,))],
        flops=2 * total * width * 700,
        moved=6 << 20,
        limit=50,
    )(
        *pieces, w_other, recv, log_rate, step_bias, query_key, value_gate, gates_proj.T,
        head_gain.reshape(1, dim), out_proj, migration, states, tok, post_gain.reshape(1, width),
    )
    swapped = core_swap(part_other)
    part = (part_own.astype(F32) + swapped.astype(F32)).astype(BF16)
    up_own = expert_up.reshape(width, -1)
    down_own = expert_down.reshape(-1, width)
    hidden = down_own.shape[0]
    part, up_out, down_out = lax.optimization_barrier((part, up_own, down_own))
    up_other = core_swap(up_out)
    down_other = core_swap(down_out)
    got = exchange(part)

    state_out = call(
        state_kernel,
        sds((rows, dim, dim), F32),
        [VMEM] * 3 + [HBM] * 2 + [VMEM],
        VMEM,
        scratch=[pltpu.SMEM((groups * rows,), jnp.int32)] + plan + [dma((2,))],
        flops=2 * total * dim * dim,
        moved=5 << 20,
    )(k_rows, w_rows, decay, migration, states, kept)

    moe, mixed = call(
        mixed_kernel,
        (sds((peers, STEPS, width), BF16), sds((STEPS, width), BF16)),
        [VMEM],
        (VMEM, VMEM),
    )(got)
    moe_rows = exchange(moe)
    served = call(
        expert_kernel,
        sds((peers, STEPS, width), BF16),
        [VMEM, ANY] + [HBM] * 4,
        VMEM,
        scratch=[
            vm((peers, 2 * STEPS, EXTRA), F32), vm((width, 2 * hidden), BF16), vm((width, 2 * hidden), BF16),
            vm((hidden, width), BF16), vm((hidden, width), BF16), dma((5,)),
        ],
        flops=1 << 29,
        moved=7 << 20,
    )(moe_rows, comb, up_own, up_other, down_own, down_other)
    back = exchange(served)
    out = call(sum_kernel, sds((STEPS, width), BF16), [VMEM] * 2, VMEM)(back, mixed)
    return (out.reshape(STEPS, 1, width), state_out.reshape(state_in.shape))


def solution(mesh):
    in_specs = (
        P(None, ("dp", "expert"), None),
        P(None, ("dp", "expert"), None),
        P(None, ("dp", "expert"), None),
        P(None, "dp"),
        P(),
        P("dp", "expert", None, None),
        P(),
        P(None, "expert"),
        P(None, "expert"),
        P(None, "expert"),
        P("expert"),
        P("expert"),
        P(),
        P("expert", None),
        P(),
        P("expert", None, None),
        P("expert", None, None),
    )
    out_specs = (P(None, ("dp", "expert"), None), P("dp", "expert", None, None))
    return jax.shard_map(body, mesh=mesh, in_specs=in_specs, out_specs=out_specs, check_vma=False)
```

```python
import functools

import jax
import jax.numpy as jnp
from jax import lax
from jax.experimental import pallas as pl
from jax.experimental.pallas import tpu as pltpu
from jax.sharding import PartitionSpec as P

F32 = jnp.float32
BF16 = jnp.bfloat16
STEPS = 4
CAP = 2
EPS = 1e-06
EXTRA = 128
VMEM = pl.BlockSpec(memory_space=pltpu.VMEM)
HBM = pl.BlockSpec(memory_space=pltpu.HBM)
ANY = pl.BlockSpec(memory_space=pl.ANY)


def core_swap(value):
    n = lax.axis_size("expert")
    return lax.ppermute(value, "expert", [(i, i ^ 1) for i in range(n)])


def hop(value, mask):
    n = lax.axis_size("expert")
    return lax.ppermute(value, "expert", [(i, i ^ mask) for i in range(n)])


def exchange(chunks):
    n = lax.axis_size("expert")
    groups = [list(range(0, n, 2)), list(range(1, n, 2))]
    return lax.all_to_all(
        chunks, "expert", split_axis=0, concat_axis=0, tiled=True, axis_index_groups=groups
    )


def call(kernel, out_shape, in_specs, out_specs, scratch=(), limit=24, flops=0, moved=0):
    return pl.pallas_call(
        kernel,
        out_shape=out_shape,
        in_specs=in_specs,
        out_specs=out_specs,
        scratch_shapes=list(scratch),
        compiler_params=pltpu.CompilerParams(vmem_limit_bytes=limit * 1024 * 1024),
        cost_estimate=pl.CostEstimate(flops=flops, bytes_accessed=moved, transcendentals=0),
    )


def fetch(sems, *pairs):
    copies = [pltpu.make_async_copy(src, dst, sems.at[i]) for i, (src, dst) in enumerate(pairs)]
    for copy in copies:
        copy.start()
    return copies


def start_kernel(
    tok, gain, ids, wts, mask, mig, states, out, parcel,
    tok_v, gain_v, ids_v, wts_v, mask_v, mig_v, loaded, sems, row_sems,
):
    groups = parcel.shape[0]
    rows = states.shape[0]
    bits = rows.bit_length() - 1
    group = lax.axis_index("dp")
    me = lax.axis_index("expert")
    copies = fetch(
        sems, (mig, mig_v), (tok, tok_v), (gain, gain_v), (ids, ids_v), (wts, wts_v), (mask, mask_v)
    )
    copies[0].wait()
    old = mig_v[...]
    lane = lax.broadcasted_iota(jnp.int32, old.shape, 0) * old.shape[1]
    lane = lane + lax.broadcasted_iota(jnp.int32, old.shape, 1)
    ours = (old >> bits) == group
    key = ((lane & (rows - 1)) * rows + (old & (rows - 1))).astype(F32)
    row_copies = []
    for g in range(groups):
        mask = ours & ((lane >> bits) == g)
        ahead = jnp.min(jnp.where(mask, key, float(rows * rows - 1)))
        behind = jnp.max(jnp.where(mask, key, 0.0))
        for slot, found in enumerate((ahead, behind)):
            k = g * CAP + slot
            copy = pltpu.make_async_copy(
                states.at[found.astype(jnp.int32) & (rows - 1)], loaded.at[k], row_sems.at[k]
            )
            copy.start()
            row_copies.append(copy)
    for copy in copies[1:]:
        copy.wait()
    x = tok_v[...].astype(F32)
    scale = lax.rsqrt(jnp.mean(x * x, axis=-1, keepdims=True) + EPS)
    normed = (x * scale * gain_v[...]).astype(BF16)
    lane = lax.broadcasted_iota(jnp.int32, (STEPS, EXTRA), 1)
    chosen = ids_v[...]
    weights = wts_v[...].astype(F32)
    comb = jnp.zeros((STEPS, EXTRA), F32)
    for k in range(chosen.shape[1]):
        comb = comb + jnp.where(lane == chosen[:, k : k + 1], weights[:, k : k + 1], 0.0)
    masks = mask_v[...].astype(F32)
    col = lax.broadcasted_iota(jnp.int32, masks.shape, 1)
    own_mask = jnp.sum(jnp.where(col == me, masks, 0.0), axis=-1, keepdims=True)
    comb = jnp.where(lane == EXTRA - 1, own_mask, comb).astype(BF16)
    width = x.shape[1]
    out[:, :width] = normed
    out[:, width:] = comb
    for k, copy in enumerate(row_copies):
        copy.wait()
        parcel[k // CAP, k % CAP] = loaded[k].astype(BF16)


def place_moved(mig_s, filled, dest, begin, moved):
    rows = begin.shape[0]
    groups = moved.shape[0]
    group = lax.axis_index("dp")
    for g in range(groups):
        filled[g] = 0
    for r in range(rows):
        g = mig_s[group * rows + r] >> (rows.bit_length() - 1)
        slot = filled[g]
        dest[CAP * g + jnp.minimum(slot, CAP - 1)] = r
        filled[g] = slot + 1
    for g in range(groups):
        for slot in range(CAP):

            @pl.when((filled[g] > slot) & (group != g))
            def _(g=g, slot=slot):
                begin[dest[CAP * g + slot]] = moved[g, slot].astype(F32)


def heads_kernel(
    p0, p1, p2, p3, p4, p5, p6, p7, w_other_v, moved, rates, w_own, w_vz, w_ab, head_gain, w_out, mig,
    states, tok, post_gain, *refs
):
    part_own, part_other, k_out, w_rows, decay_out, comb_out, keep = refs[:7]
    (
        w_own_v, w_vz_v, w_ab_v, rates_v, gain_v, w_out_v, mig_s, begin, tok_v, post_v,
        kq, ks, qs, q_all, v_all, z_all, d_all, b_all, m_all, h_all, dest, filled, sems,
    ) = refs[7:]
    rows = states.shape[0]
    dim = states.shape[1]
    total = rows * STEPS
    width = w_own.shape[0]
    copies = fetch(
        sems, (w_own, w_own_v), (w_vz, w_vz_v),
        (w_ab, w_ab_v), (rates, rates_v), (mig, mig_s), (states, begin),
        (head_gain, gain_v), (w_out, w_out_v), (tok, tok_v), (post_gain, post_v),
        (moved, keep),
    )
    pieces = (p0, p1, p2, p3, p4, p5, p6, p7)
    x = jnp.concatenate([piece[:, :width] for piece in pieces], axis=0)
    extra = jnp.concatenate([piece[:, width:] for piece in pieces], axis=0).astype(F32)
    live = extra[:, EXTRA - 1 :]
    second = jnp.dot(x, w_other_v[...], preferred_element_type=F32)
    copies[0].wait()
    first = jnp.dot(x, w_own_v[...], preferred_element_type=F32)
    copies[1].wait()
    vz = jnp.dot(x, w_vz_v[...], preferred_element_type=F32)
    for copy in copies[2:4]:
        copy.wait()
    ab = lax.dot_general(
        x, w_ab_v[...], (((1,), (1,)), ((), ())), preferred_element_type=F32
    )
    me = lax.axis_index("expert")
    even = me % 2 == 0
    q = jnp.where(even, first, second)
    k = jnp.where(even, second, first)
    q = q * (lax.rsqrt(jnp.sum(q * q, axis=-1, keepdims=True) + EPS) * dim**-0.5)
    k = k * lax.rsqrt(jnp.sum(k * k, axis=-1, keepdims=True) + EPS)
    beta = jax.nn.sigmoid(ab[:, 1:2])
    rate = jnp.exp(rates_v[0:1, 0:1])
    drive = ab[:, 0:1] + rates_v[1:2, 0:1]
    soft = jnp.maximum(drive, 0.0) + jnp.log1p(jnp.exp(-jnp.abs(drive)))
    decay = jnp.exp(-rate * soft)
    wide = (total, dim)
    q_all[...] = q
    k_out[...] = k
    v_all[...] = vz[:, :dim]
    z_all[...] = vz[:, dim:]
    d_all[...] = jnp.broadcast_to(decay, wide)
    b_all[...] = jnp.broadcast_to(beta, wide)
    m_all[...] = jnp.broadcast_to(live, wide)
    for s in range(rows):
        kq[8 * s : 8 * s + 4] = k[4 * s : 4 * s + 4]
        kq[8 * s + 4 : 8 * s + 8] = q[4 * s : 4 * s + 4]
    for copy in copies[4:]:
        copy.wait()
    place_moved(mig_s, filled, dest, begin, moved)
    for s in range(rows):
        r = me ^ (2 * (s % (rows // 2)) + s // (rows // 2))
        both = jnp.dot(
            kq[8 * s : 8 * s + 8].astype(BF16), begin[r].astype(BF16), preferred_element_type=F32
        )
        ks[4 * s : 4 * s + 4] = both[:4]
        qs[4 * s : 4 * s + 4] = both[4:]

    def at(ref, t):
        return ref[pl.ds(t, rows, stride=STEPS), :]

    kept = jnp.ones((rows, dim), F32)
    past = []
    gain = gain_v[...]
    for t in range(STEPS):
        k_t, q_t, d_t, m_t = at(k_out, t), at(q_all, t), at(d_all, t), at(m_all, t)
        k_state = kept * at(ks, t)
        q_state = kept * at(qs, t)
        for k_s, w_s in past:
            k_state = k_state + jnp.sum(k_t * k_s, axis=-1, keepdims=True) * w_s
            q_state = q_state + jnp.sum(q_t * k_s, axis=-1, keepdims=True) * w_s
        write = at(b_all, t) * (at(v_all, t) - d_t * k_state)
        o = d_t * q_state + jnp.sum(q_t * k_t, axis=-1, keepdims=True) * write
        scale = lax.rsqrt(jnp.mean(o * o, axis=-1, keepdims=True) + EPS)
        z_t = at(z_all, t)
        h_all[pl.ds(t, rows, stride=STEPS), :] = o * scale * gain * (z_t * jax.nn.sigmoid(z_t))
        alive = m_t > 0.5
        a_t = jnp.where(alive, d_t, 1.0)
        kept = kept * a_t
        past = [(k_s, w_s * a_t) for k_s, w_s in past] + [(k_t, jnp.where(alive, write, 0.0))]
    for t in range(STEPS):
        w_rows[pl.ds(t, rows, stride=STEPS), :] = past[t][1]
    decay_out[...] = kept
    part = jnp.dot(h_all[...].astype(BF16), w_out_v[...], preferred_element_type=F32)
    for u in range(rows // 2):
        chip = (me // 2) ^ u
        own = part[STEPS * u : STEPS * (u + 1)]
        if u == 0:
            own = own + tok_v[...].astype(F32)
        part_own[chip] = own.astype(BF16)
        part_other[chip] = part[STEPS * (rows // 2 + u) : STEPS * (rows // 2 + u + 1)].astype(BF16)
        comb_out[chip, :STEPS] = extra[STEPS * u : STEPS * (u + 1)]
        comb_out[u, STEPS : STEPS + 1] = post_v[:, EXTRA * u : EXTRA * (u + 1)]


def state_kernel(k_in, w_rows, decay, mig, states, *refs):
    moved, out, mig_s, dest, filled, sems = refs
    rows = states.shape[0]
    copies = fetch(
        sems, (mig, mig_s), (states, out)
    )
    for copy in copies:
        copy.wait()
    place_moved(mig_s, filled, dest, out, moved)
    me = lax.axis_index("expert")
    for s in range(rows):
        r = me ^ (2 * (s % (rows // 2)) + s // (rows // 2))
        k_s = k_in[4 * s : 4 * s + 4, :]
        w_s = w_rows[4 * s : 4 * s + 4, :]
        outer = lax.dot_general(k_s, w_s, (((0,), (0,)), ((), ())), preferred_element_type=F32)
        out[r] = decay[s : s + 1, :] * out[r] + outer


def mixed_kernel(got, out, mixed_out):
    mixed = jnp.sum(got[...].astype(F32), axis=0).astype(BF16)
    mixed_out[...] = mixed
    m = mixed.astype(F32)
    scale = lax.rsqrt(jnp.mean(m * m, axis=-1, keepdims=True) + EPS)
    normed = (m * scale).astype(BF16)
    for j in range(out.shape[0]):
        out[j] = normed


def expert_kernel(
    rows_in, extra_v, up_own_v, up_other_v, down_own_v, down_other_v, out
):
    half = rows_in.shape[0] * STEPS
    me = lax.axis_index("expert")
    partner = me + 1 - 2 * (me % 2)
    extra = extra_v[...]
    gain = jnp.concatenate([extra[j, STEPS : STEPS + 1] for j in range(extra.shape[0])], axis=1)
    x = (rows_in[...].astype(F32).reshape(half, -1) * gain).astype(BF16)
    comb = extra[:, :STEPS].reshape(half, EXTRA)
    lane = lax.broadcasted_iota(jnp.int32, comb.shape, 1)
    total = None
    for index, up, down in ((me, up_own_v, down_own_v), (partner, up_other_v, down_other_v)):
        hidden = down.shape[0]
        proj = jnp.dot(x, up[...], preferred_element_type=F32)
        g, u = proj[:, :hidden], proj[:, hidden:]
        act = (g * jax.nn.sigmoid(g) * u).astype(BF16)
        weight = jnp.sum(jnp.where(lane == index, comb, 0.0), axis=-1, keepdims=True)
        result = weight * jnp.dot(act, down[...], preferred_element_type=F32)
        total = result if total is None else total + result
    total = total.astype(BF16)
    for j in range(out.shape[0]):
        out[j] = total[STEPS * j : STEPS * (j + 1)]


def sum_kernel(got, mixed, out):
    out[...] = (mixed[...].astype(F32) + jnp.sum(got[...].astype(F32), axis=0)).astype(BF16)


def body(
    tokens, route_ids, route_weights, active_mask, migration, state_in, in_gain, query_key,
    value_gate, gates_proj, log_rate, step_bias, head_gain, out_proj, post_gain, expert_up,
    expert_down,
):
    groups = lax.axis_size("dp")
    members = lax.axis_size("expert")
    rows = state_in.shape[0]
    dim = state_in.shape[2]
    width = tokens.shape[2]
    peers = members // 2
    half = rows * STEPS // 2
    total = rows * STEPS
    sds = jax.ShapeDtypeStruct
    vm = pltpu.VMEM
    dma = pltpu.SemaphoreType.DMA
    tok = tokens.reshape(STEPS, width)
    states = state_in.reshape(rows, dim, dim)
    top = route_ids.shape[2]

    w_other = core_swap(query_key)
    payload, parcel = call(
        start_kernel,
        (sds((STEPS, width + EXTRA), BF16), sds((groups, CAP, dim, dim), BF16)),
        [HBM] * 7,
        (VMEM, VMEM),
        scratch=[
            vm((STEPS, width), BF16), vm((1, width), F32), vm((STEPS, top), jnp.int32),
            vm((STEPS, top), BF16), vm((STEPS, rows), jnp.int32),
            vm((groups * rows // 128, 128), jnp.int32), vm((groups * CAP, dim, dim), F32),
            dma((6,)), dma((groups * CAP,)),
        ],
        limit=60,
    )(
        tok, in_gain.reshape(1, width), route_ids.reshape(STEPS, top),
        route_weights.reshape(STEPS, top), active_mask, migration.reshape(-1, 128), states,
    )
    recv = lax.all_to_all(parcel, "dp", split_axis=0, concat_axis=0, tiled=True)
    line = jnp.concatenate([payload] + [hop(payload, m) for m in (2, 4, 6)])
    rates = jnp.broadcast_to(jnp.concatenate([log_rate, step_bias])[:, None], (2, dim))
    line, rates = lax.optimization_barrier((line, rates))
    pieces = [line] + [hop(line, m) for m in (8, 16, 24)]
    pieces = pieces + [core_swap(piece) for piece in pieces]

    tall = vm((total, dim), F32)
    plan = [pltpu.SMEM((groups * CAP,), jnp.int32), pltpu.SMEM((groups,), jnp.int32)]
    part_own, part_other, k_rows, w_rows, decay, comb, kept = call(
        heads_kernel,
        (
            sds((peers, STEPS, width), BF16), sds((peers, STEPS, width), BF16),
            sds((total, dim), F32), sds((total, dim), F32), sds((rows, dim), F32),
            sds((peers, 2 * STEPS, EXTRA), F32), sds((groups, CAP, dim, dim), BF16),
        ),
        [VMEM] * 10 + [ANY] + [HBM] * 9,
        (VMEM,) * 6 + (HBM,),
        scratch=[
            vm((width, dim), BF16), vm((width, 2 * dim), BF16), vm((2, width), BF16),
            vm((2, dim), F32),
            vm((1, dim), F32), vm((dim, width), BF16), pltpu.SMEM((groups * rows,), jnp.int32),
            vm((rows, dim, dim), F32), vm((STEPS, width), BF16), vm((1, width), F32),
            vm((2 * total, dim), F32),
        ] + [tall] * 9 + plan + [dma((11,))],
        flops=2 * total * width * 700,
        moved=6 << 20,
        limit=50,
    )(
        *pieces, w_other, recv, rates, query_key, value_gate, gates_proj.T,
        head_gain.reshape(1, dim), out_proj, migration, states, tok, post_gain.reshape(1, width),
    )
    swapped = core_swap(part_other)
    part = (part_own.astype(F32) + swapped.astype(F32)).astype(BF16)
    up_own = expert_up.reshape(width, -1)
    down_own = expert_down.reshape(-1, width)
    hidden = down_own.shape[0]
    part, up_out, down_out = lax.optimization_barrier((part, up_own, down_own))
    up_other = core_swap(up_out)
    down_other = core_swap(down_out)
    got = exchange(part)

    state_out = call(
        state_kernel,
        sds((rows, dim, dim), F32),
        [VMEM] * 3 + [HBM] * 2 + [VMEM],
        VMEM,
        scratch=[pltpu.SMEM((groups * rows,), jnp.int32)] + plan + [dma((2,))],
        flops=2 * total * dim * dim,
        moved=5 << 20,
    )(k_rows, w_rows, decay, migration, states, kept)

    moe, mixed = call(
        mixed_kernel,
        (sds((peers, STEPS, width), BF16), sds((STEPS, width), BF16)),
        [VMEM],
        (VMEM, VMEM),
    )(got)
    moe_rows = exchange(moe)
    served = call(
        expert_kernel,
        sds((peers, STEPS, width), BF16),
        [VMEM] * 6,
        VMEM,
        flops=1 << 29,
        moved=7 << 20,
        limit=10,
    )(moe_rows, comb, up_own, up_other, down_own, down_other)
    back = exchange(served)
    out = call(sum_kernel, sds((STEPS, width), BF16), [VMEM] * 2, VMEM)(back, mixed)
    return (out.reshape(STEPS, 1, width), state_out.reshape(state_in.shape))


def solution(mesh):
    in_specs = (
        P(None, ("dp", "expert"), None),
        P(None, ("dp", "expert"), None),
        P(None, ("dp", "expert"), None),
        P(None, "dp"),
        P(),
        P("dp", "expert", None, None),
        P(),
        P(None, "expert"),
        P(None, "expert"),
        P(None, "expert"),
        P("expert"),
        P("expert"),
        P(),
        P("expert", None),
        P(),
        P("expert", None, None),
        P("expert", None, None),
    )
    out_specs = (P(None, ("dp", "expert"), None), P("dp", "expert", None, None))
    return jax.shard_map(body, mesh=mesh, in_specs=in_specs, out_specs=out_specs, check_vma=False)
```

```python
import functools

import jax
import jax.numpy as jnp
from jax import lax
from jax.experimental import pallas as pl
from jax.experimental.pallas import tpu as pltpu
from jax.sharding import PartitionSpec as P

F32 = jnp.float32
BF16 = jnp.bfloat16
STEPS = 4
CAP = 2
EPS = 1e-06
EXTRA = 128
VMEM = pl.BlockSpec(memory_space=pltpu.VMEM)
HBM = pl.BlockSpec(memory_space=pltpu.HBM)
ANY = pl.BlockSpec(memory_space=pl.ANY)


def core_swap(value):
    n = lax.axis_size("expert")
    return lax.ppermute(value, "expert", [(i, i ^ 1) for i in range(n)])


def hop(value, mask):
    n = lax.axis_size("expert")
    return lax.ppermute(value, "expert", [(i, i ^ mask) for i in range(n)])


def exchange(chunks):
    n = lax.axis_size("expert")
    groups = [list(range(0, n, 2)), list(range(1, n, 2))]
    return lax.all_to_all(
        chunks, "expert", split_axis=0, concat_axis=0, tiled=True, axis_index_groups=groups
    )


def call(kernel, out_shape, in_specs, out_specs, scratch=(), limit=24, flops=0, moved=0):
    return pl.pallas_call(
        kernel,
        out_shape=out_shape,
        in_specs=in_specs,
        out_specs=out_specs,
        scratch_shapes=list(scratch),
        compiler_params=pltpu.CompilerParams(vmem_limit_bytes=limit * 1024 * 1024),
        cost_estimate=pl.CostEstimate(flops=flops, bytes_accessed=moved, transcendentals=0),
    )


def fetch(sems, *pairs):
    copies = [pltpu.make_async_copy(src, dst, sems.at[i]) for i, (src, dst) in enumerate(pairs)]
    for copy in copies:
        copy.start()
    return copies


def start_kernel(
    tok, gain, ids, wts, mask, mig, states, out, parcel,
    tok_v, gain_v, ids_v, wts_v, mask_v, mig_v, loaded, sems, row_sems,
):
    groups = parcel.shape[0]
    rows = states.shape[0]
    bits = rows.bit_length() - 1
    group = lax.axis_index("dp")
    me = lax.axis_index("expert")
    copies = fetch(
        sems, (mig, mig_v), (tok, tok_v), (gain, gain_v), (ids, ids_v), (wts, wts_v), (mask, mask_v)
    )
    copies[0].wait()
    old = mig_v[...]
    lane = lax.broadcasted_iota(jnp.int32, old.shape, 0) * old.shape[1]
    lane = lane + lax.broadcasted_iota(jnp.int32, old.shape, 1)
    ours = (old >> bits) == group
    key = ((lane & (rows - 1)) * rows + (old & (rows - 1))).astype(F32)
    found = []
    for g in range(groups):
        mask = ours & ((lane >> bits) == g)
        found.append(jnp.min(jnp.where(mask, key, float(rows * rows - 1))))
        found.append(jnp.max(jnp.where(mask, key, 0.0)))
    picked = [value.astype(jnp.int32) & (rows - 1) for value in found]
    row_copies = []
    for k, row in enumerate(picked):
        copy = pltpu.make_async_copy(states.at[row], loaded.at[k], row_sems.at[k])
        copy.start()
        row_copies.append(copy)
    for copy in copies[1:]:
        copy.wait()
    x = tok_v[...].astype(F32)
    scale = lax.rsqrt(jnp.mean(x * x, axis=-1, keepdims=True) + EPS)
    normed = (x * scale * gain_v[...]).astype(BF16)
    lane = lax.broadcasted_iota(jnp.int32, (STEPS, EXTRA), 1)
    chosen = ids_v[...]
    weights = wts_v[...].astype(F32)
    comb = jnp.zeros((STEPS, EXTRA), F32)
    for k in range(chosen.shape[1]):
        comb = comb + jnp.where(lane == chosen[:, k : k + 1], weights[:, k : k + 1], 0.0)
    masks = mask_v[...].astype(F32)
    col = lax.broadcasted_iota(jnp.int32, masks.shape, 1)
    own_mask = jnp.sum(jnp.where(col == me, masks, 0.0), axis=-1, keepdims=True)
    comb = jnp.where(lane == EXTRA - 1, own_mask, comb).astype(BF16)
    width = x.shape[1]
    out[:, :width] = normed
    out[:, width:] = comb
    for k, copy in enumerate(row_copies):
        copy.wait()
        parcel[k // CAP, k % CAP] = loaded[k].astype(BF16)


def place_moved(mig_s, filled, dest, begin, moved):
    rows = begin.shape[0]
    groups = moved.shape[0]
    group = lax.axis_index("dp")
    for g in range(groups):
        filled[g] = 0
    for r in range(rows):
        g = mig_s[group * rows + r] >> (rows.bit_length() - 1)
        slot = filled[g]
        dest[CAP * g + jnp.minimum(slot, CAP - 1)] = r
        filled[g] = slot + 1
    for g in range(groups):
        for slot in range(CAP):

            @pl.when((filled[g] > slot) & (group != g))
            def _(g=g, slot=slot):
                begin[dest[CAP * g + slot]] = moved[g, slot].astype(F32)


def heads_kernel(
    p0, p1, p2, p3, p4, p5, p6, p7, w_other_v, moved, w_own_v, rates, w_vz, w_ab, head_gain, w_out, mig,
    states, tok, post_gain, *refs
):
    part_own, part_other, k_out, w_rows, decay_out, comb_out, keep = refs[:7]
    (
        w_vz_v, w_ab_v, rates_v, gain_v, w_out_v, mig_s, begin, tok_v, post_v,
        kq, ks, qs, q_all, v_all, z_all, d_all, b_all, m_all, h_all, dest, filled, sems,
    ) = refs[7:]
    rows = states.shape[0]
    dim = states.shape[1]
    total = rows * STEPS
    width = w_own_v.shape[0]
    copies = fetch(
        sems, (w_vz, w_vz_v),
        (w_ab, w_ab_v), (rates, rates_v), (mig, mig_s), (states, begin),
        (head_gain, gain_v), (w_out, w_out_v), (tok, tok_v), (post_gain, post_v),
        (moved, keep),
    )
    pieces = (p0, p1, p2, p3, p4, p5, p6, p7)
    x = jnp.concatenate([piece[:, :width] for piece in pieces], axis=0)
    extra = jnp.concatenate([piece[:, width:] for piece in pieces], axis=0).astype(F32)
    live = extra[:, EXTRA - 1 :]
    second = jnp.dot(x, w_other_v[...], preferred_element_type=F32)
    first = jnp.dot(x, w_own_v[...], preferred_element_type=F32)
    copies[0].wait()
    vz = jnp.dot(x, w_vz_v[...], preferred_element_type=F32)
    for copy in copies[1:3]:
        copy.wait()
    ab = lax.dot_general(
        x, w_ab_v[...], (((1,), (1,)), ((), ())), preferred_element_type=F32
    )
    me = lax.axis_index("expert")
    even = me % 2 == 0
    q = jnp.where(even, first, second)
    k = jnp.where(even, second, first)
    q = q * (lax.rsqrt(jnp.sum(q * q, axis=-1, keepdims=True) + EPS) * dim**-0.5)
    k = k * lax.rsqrt(jnp.sum(k * k, axis=-1, keepdims=True) + EPS)
    beta = jax.nn.sigmoid(ab[:, 1:2])
    rate = jnp.exp(rates_v[0:1, 0:1])
    drive = ab[:, 0:1] + rates_v[1:2, 0:1]
    soft = jnp.maximum(drive, 0.0) + jnp.log1p(jnp.exp(-jnp.abs(drive)))
    decay = jnp.exp(-rate * soft)
    wide = (total, dim)
    q_all[...] = q
    k_out[...] = k
    v_all[...] = vz[:, :dim]
    z_all[...] = vz[:, dim:]
    d_all[...] = jnp.broadcast_to(decay, wide)
    b_all[...] = jnp.broadcast_to(beta, wide)
    m_all[...] = jnp.broadcast_to(live, wide)
    for s in range(rows):
        kq[8 * s : 8 * s + 4] = k[4 * s : 4 * s + 4]
        kq[8 * s + 4 : 8 * s + 8] = q[4 * s : 4 * s + 4]
    for copy in copies[3:]:
        copy.wait()
    place_moved(mig_s, filled, dest, begin, moved)
    for s in range(rows):
        r = me ^ (2 * (s % (rows // 2)) + s // (rows // 2))
        both = jnp.dot(
            kq[8 * s : 8 * s + 8].astype(BF16), begin[r].astype(BF16), preferred_element_type=F32
        )
        ks[4 * s : 4 * s + 4] = both[:4]
        qs[4 * s : 4 * s + 4] = both[4:]

    def at(ref, t):
        return ref[pl.ds(t, rows, stride=STEPS), :]

    kept = jnp.ones((rows, dim), F32)
    past = []
    gain = gain_v[...]
    for t in range(STEPS):
        k_t, q_t, d_t, m_t = at(k_out, t), at(q_all, t), at(d_all, t), at(m_all, t)
        k_state = kept * at(ks, t)
        q_state = kept * at(qs, t)
        for k_s, w_s in past:
            k_state = k_state + jnp.sum(k_t * k_s, axis=-1, keepdims=True) * w_s
            q_state = q_state + jnp.sum(q_t * k_s, axis=-1, keepdims=True) * w_s
        write = at(b_all, t) * (at(v_all, t) - d_t * k_state)
        o = d_t * q_state + jnp.sum(q_t * k_t, axis=-1, keepdims=True) * write
        scale = lax.rsqrt(jnp.mean(o * o, axis=-1, keepdims=True) + EPS)
        z_t = at(z_all, t)
        h_all[pl.ds(t, rows, stride=STEPS), :] = o * scale * gain * (z_t * jax.nn.sigmoid(z_t))
        alive = m_t > 0.5
        a_t = jnp.where(alive, d_t, 1.0)
        kept = kept * a_t
        past = [(k_s, w_s * a_t) for k_s, w_s in past] + [(k_t, jnp.where(alive, write, 0.0))]
    for t in range(STEPS):
        w_rows[pl.ds(t, rows, stride=STEPS), :] = past[t][1]
    decay_out[...] = kept
    part = jnp.dot(h_all[...].astype(BF16), w_out_v[...], preferred_element_type=F32)
    for u in range(rows // 2):
        chip = (me // 2) ^ u
        own = part[STEPS * u : STEPS * (u + 1)]
        if u == 0:
            own = own + tok_v[...].astype(F32)
        part_own[chip] = own.astype(BF16)
        part_other[chip] = part[STEPS * (rows // 2 + u) : STEPS * (rows // 2 + u + 1)].astype(BF16)
        comb_out[chip, :STEPS] = extra[STEPS * u : STEPS * (u + 1)]
        comb_out[u, STEPS : STEPS + 1] = post_v[:, EXTRA * u : EXTRA * (u + 1)]


def state_kernel(k_in, w_rows, decay, mig, states, *refs):
    moved, out, mig_s, dest, filled, sems = refs
    rows = states.shape[0]
    copies = fetch(
        sems, (mig, mig_s), (states, out)
    )
    for copy in copies:
        copy.wait()
    place_moved(mig_s, filled, dest, out, moved)
    me = lax.axis_index("expert")
    for s in range(rows):
        r = me ^ (2 * (s % (rows // 2)) + s // (rows // 2))
        k_s = k_in[4 * s : 4 * s + 4, :]
        w_s = w_rows[4 * s : 4 * s + 4, :]
        outer = lax.dot_general(k_s, w_s, (((0,), (0,)), ((), ())), preferred_element_type=F32)
        out[r] = decay[s : s + 1, :] * out[r] + outer


def mixed_kernel(got, out, mixed_out):
    mixed = jnp.sum(got[...].astype(F32), axis=0).astype(BF16)
    mixed_out[...] = mixed
    m = mixed.astype(F32)
    scale = lax.rsqrt(jnp.mean(m * m, axis=-1, keepdims=True) + EPS)
    normed = (m * scale).astype(BF16)
    for j in range(out.shape[0]):
        out[j] = normed


def expert_kernel(
    rows_in, extra_v, up_own_v, up_other_v, down_own_v, down_other_v, out
):
    half = rows_in.shape[0] * STEPS
    me = lax.axis_index("expert")
    partner = me + 1 - 2 * (me % 2)
    extra = extra_v[...]
    gain = jnp.concatenate([extra[j, STEPS : STEPS + 1] for j in range(extra.shape[0])], axis=1)
    x = (rows_in[...].astype(F32).reshape(half, -1) * gain).astype(BF16)
    comb = extra[:, :STEPS].reshape(half, EXTRA)
    lane = lax.broadcasted_iota(jnp.int32, comb.shape, 1)
    total = None
    for index, up, down in ((me, up_own_v, down_own_v), (partner, up_other_v, down_other_v)):
        hidden = down.shape[0]
        proj = jnp.dot(x, up[...], preferred_element_type=F32)
        g, u = proj[:, :hidden], proj[:, hidden:]
        act = (g * jax.nn.sigmoid(g) * u).astype(BF16)
        weight = jnp.sum(jnp.where(lane == index, comb, 0.0), axis=-1, keepdims=True)
        result = weight * jnp.dot(act, down[...], preferred_element_type=F32)
        total = result if total is None else total + result
    total = total.astype(BF16)
    for j in range(out.shape[0]):
        out[j] = total[STEPS * j : STEPS * (j + 1)]


def sum_kernel(got, mixed, out):
    out[...] = (mixed[...].astype(F32) + jnp.sum(got[...].astype(F32), axis=0)).astype(BF16)


def body(
    tokens, route_ids, route_weights, active_mask, migration, state_in, in_gain, query_key,
    value_gate, gates_proj, log_rate, step_bias, head_gain, out_proj, post_gain, expert_up,
    expert_down,
):
    groups = lax.axis_size("dp")
    members = lax.axis_size("expert")
    rows = state_in.shape[0]
    dim = state_in.shape[2]
    width = tokens.shape[2]
    peers = members // 2
    half = rows * STEPS // 2
    total = rows * STEPS
    sds = jax.ShapeDtypeStruct
    vm = pltpu.VMEM
    dma = pltpu.SemaphoreType.DMA
    tok = tokens.reshape(STEPS, width)
    states = state_in.reshape(rows, dim, dim)
    top = route_ids.shape[2]

    w_other = core_swap(query_key)
    payload, parcel = call(
        start_kernel,
        (vm((STEPS, width + EXTRA), BF16), vm((groups, CAP, dim, dim), BF16)),
        [HBM] * 7,
        (VMEM, VMEM),
        scratch=[
            vm((STEPS, width), BF16), vm((1, width), F32), vm((STEPS, top), jnp.int32),
            vm((STEPS, top), BF16), vm((STEPS, rows), jnp.int32),
            vm((groups * rows // 128, 128), jnp.int32), vm((groups * CAP, dim, dim), F32),
            dma((6,)), dma((groups * CAP,)),
        ],
        limit=60,
    )(
        tok, in_gain.reshape(1, width), route_ids.reshape(STEPS, top),
        route_weights.reshape(STEPS, top), active_mask, migration.reshape(-1, 128), states,
    )
    recv = lax.all_to_all(parcel, "dp", split_axis=0, concat_axis=0, tiled=True)
    line = jnp.concatenate([payload] + [hop(payload, m) for m in (2, 4, 6)])
    rates = jnp.broadcast_to(jnp.concatenate([log_rate, step_bias])[:, None], (2, dim))
    pieces = [line] + [hop(line, m) for m in (8, 16, 24)]
    pieces[1], rates = lax.optimization_barrier((pieces[1], rates))
    pieces = pieces + [core_swap(piece) for piece in pieces]

    tall = vm((total, dim), F32)
    plan = [pltpu.SMEM((groups * CAP,), jnp.int32), pltpu.SMEM((groups,), jnp.int32)]
    part_own, part_other, k_rows, w_rows, decay, comb, kept = call(
        heads_kernel,
        (
            sds((peers, STEPS, width), BF16), sds((peers, STEPS, width), BF16),
            sds((total, dim), F32), sds((total, dim), F32), sds((rows, dim), F32),
            sds((peers, 2 * STEPS, EXTRA), F32), sds((groups, CAP, dim, dim), BF16),
        ),
        [VMEM] * 11 + [ANY] + [HBM] * 8,
        (VMEM,) * 6 + (HBM,),
        scratch=[
            vm((width, 2 * dim), BF16), vm((2, width), BF16),
            vm((2, dim), F32),
            vm((1, dim), F32), vm((dim, width), BF16), pltpu.SMEM((groups * rows,), jnp.int32),
            vm((rows, dim, dim), F32), vm((STEPS, width), BF16), vm((1, width), F32),
            vm((2 * total, dim), F32),
        ] + [tall] * 9 + plan + [dma((10,))],
        flops=2 * total * width * 700,
        moved=6 << 20,
        limit=50,
    )(
        *pieces, w_other, recv, query_key, rates, value_gate, gates_proj.T,
        head_gain.reshape(1, dim), out_proj, migration, states, tok, post_gain.reshape(1, width),
    )
    swapped = core_swap(part_other)
    part = (part_own.astype(F32) + swapped.astype(F32)).astype(BF16)
    up_own = expert_up.reshape(width, -1)
    down_own = expert_down.reshape(-1, width)
    hidden = down_own.shape[0]
    part, up_out, down_out = lax.optimization_barrier((part, up_own, down_own))
    up_other = core_swap(up_out)
    down_other = core_swap(down_out)
    got = exchange(part)

    state_out = call(
        state_kernel,
        sds((rows, dim, dim), F32),
        [VMEM] * 3 + [HBM] * 2 + [VMEM],
        VMEM,
        scratch=[pltpu.SMEM((groups * rows,), jnp.int32)] + plan + [dma((2,))],
        flops=2 * total * dim * dim,
        moved=5 << 20,
    )(k_rows, w_rows, decay, migration, states, kept)

    moe, mixed = call(
        mixed_kernel,
        (sds((peers, STEPS, width), BF16), sds((STEPS, width), BF16)),
        [VMEM],
        (VMEM, VMEM),
    )(got)
    moe_rows = exchange(moe)
    served = call(
        expert_kernel,
        vm((peers, STEPS, width), BF16),
        [VMEM] * 6,
        VMEM,
        flops=1 << 29,
        moved=7 << 20,
        limit=10,
    )(moe_rows, comb, up_own, up_other, down_own, down_other)
    back = exchange(served)
    out = call(sum_kernel, sds((STEPS, width), BF16), [VMEM] * 2, VMEM)(back, mixed)
    return (out.reshape(STEPS, 1, width), state_out.reshape(state_in.shape))


def solution(mesh):
    in_specs = (
        P(None, ("dp", "expert"), None),
        P(None, ("dp", "expert"), None),
        P(None, ("dp", "expert"), None),
        P(None, "dp"),
        P(),
        P("dp", "expert", None, None),
        P(),
        P(None, "expert"),
        P(None, "expert"),
        P(None, "expert"),
        P("expert"),
        P("expert"),
        P(),
        P("expert", None),
        P(),
        P("expert", None, None),
        P("expert", None, None),
    )
    out_specs = (P(None, ("dp", "expert"), None), P("dp", "expert", None, None))
    return jax.shard_map(body, mesh=mesh, in_specs=in_specs, out_specs=out_specs, check_vma=False)
```

```python
import functools

import jax
import jax.numpy as jnp
from jax import lax
from jax.experimental import pallas as pl
from jax.experimental.pallas import tpu as pltpu
from jax.sharding import PartitionSpec as P

F32 = jnp.float32
BF16 = jnp.bfloat16
STEPS = 4
CAP = 2
EPS = 1e-06
EXTRA = 128
VMEM = pl.BlockSpec(memory_space=pltpu.VMEM)
HBM = pl.BlockSpec(memory_space=pltpu.HBM)
ANY = pl.BlockSpec(memory_space=pl.ANY)


def core_swap(value):
    n = lax.axis_size("expert")
    return lax.ppermute(value, "expert", [(i, i ^ 1) for i in range(n)])


def hop(value, mask):
    n = lax.axis_size("expert")
    return lax.ppermute(value, "expert", [(i, i ^ mask) for i in range(n)])


def exchange(chunks):
    n = lax.axis_size("expert")
    groups = [list(range(0, n, 2)), list(range(1, n, 2))]
    return lax.all_to_all(
        chunks, "expert", split_axis=0, concat_axis=0, tiled=True, axis_index_groups=groups
    )


def call(kernel, out_shape, in_specs, out_specs, scratch=(), limit=24, flops=0, moved=0):
    return pl.pallas_call(
        kernel,
        out_shape=out_shape,
        in_specs=in_specs,
        out_specs=out_specs,
        scratch_shapes=list(scratch),
        compiler_params=pltpu.CompilerParams(vmem_limit_bytes=limit * 1024 * 1024),
        cost_estimate=pl.CostEstimate(flops=flops, bytes_accessed=moved, transcendentals=0),
    )


def fetch(sems, *pairs):
    copies = [pltpu.make_async_copy(src, dst, sems.at[i]) for i, (src, dst) in enumerate(pairs)]
    for copy in copies:
        copy.start()
    return copies


def start_kernel(
    tok, gain, ids, wts, mask, mig, states, out, parcel,
    tok_v, gain_v, ids_v, wts_v, mask_v, mig_v, loaded, sems, row_sems,
):
    groups = parcel.shape[0]
    rows = states.shape[0]
    bits = rows.bit_length() - 1
    group = lax.axis_index("dp")
    me = lax.axis_index("expert")
    copies = fetch(
        sems, (mig, mig_v), (tok, tok_v), (gain, gain_v), (ids, ids_v), (wts, wts_v), (mask, mask_v)
    )
    copies[0].wait()
    old = mig_v[...]
    lane = lax.broadcasted_iota(jnp.int32, old.shape, 0) * old.shape[1]
    lane = lane + lax.broadcasted_iota(jnp.int32, old.shape, 1)
    ours = (old >> bits) == group
    key = ((lane & (rows - 1)) * rows + (old & (rows - 1))).astype(F32)
    found = []
    for g in range(groups):
        mask = ours & ((lane >> bits) == g)
        found.append(jnp.min(jnp.where(mask, key, float(rows * rows - 1))))
        found.append(jnp.max(jnp.where(mask, key, 0.0)))
    picked = [value.astype(jnp.int32) & (rows - 1) for value in found]
    row_copies = []
    for k, row in enumerate(picked):
        copy = pltpu.make_async_copy(states.at[row], loaded.at[k], row_sems.at[k])
        copy.start()
        row_copies.append(copy)
    for copy in copies[1:]:
        copy.wait()
    x = tok_v[...].astype(F32)
    scale = lax.rsqrt(jnp.mean(x * x, axis=-1, keepdims=True) + EPS)
    normed = (x * scale * gain_v[...]).astype(BF16)
    lane = lax.broadcasted_iota(jnp.int32, (STEPS, EXTRA), 1)
    chosen = ids_v[...]
    weights = wts_v[...].astype(F32)
    comb = jnp.zeros((STEPS, EXTRA), F32)
    for k in range(chosen.shape[1]):
        comb = comb + jnp.where(lane == chosen[:, k : k + 1], weights[:, k : k + 1], 0.0)
    masks = mask_v[...].astype(F32)
    col = lax.broadcasted_iota(jnp.int32, masks.shape, 1)
    own_mask = jnp.sum(jnp.where(col == me, masks, 0.0), axis=-1, keepdims=True)
    comb = jnp.where(lane == EXTRA - 1, own_mask, comb).astype(BF16)
    width = x.shape[1]
    out[:, :width] = normed
    out[:, width:] = comb
    for k, copy in enumerate(row_copies):
        copy.wait()
        parcel[k // CAP, k % CAP] = loaded[k].astype(BF16)


def plan_moved(mig_s, filled, dest, rows, groups):
    group = lax.axis_index("dp")
    for g in range(groups):
        filled[g] = 0
    for r in range(rows):
        g = mig_s[group * rows + r] >> (rows.bit_length() - 1)
        slot = filled[g]
        dest[CAP * g + jnp.minimum(slot, CAP - 1)] = r
        filled[g] = slot + 1

def place_moved(filled, dest, begin, moved):
    group = lax.axis_index("dp")
    groups = moved.shape[0]
    for g in range(groups):
        for slot in range(CAP):

            @pl.when((filled[g] > slot) & (group != g))
            def _(g=g, slot=slot):
                begin[dest[CAP * g + slot]] = moved[g, slot].astype(F32)


def heads_kernel(
    p0, p1, p2, p3, p4, p5, p6, p7, w_other_v, moved, w_own_v, rates, w_vz, w_ab, head_gain, w_out, mig,
    states, tok, post_gain, *refs
):
    part_own, part_other, k_out, w_rows, decay_out, comb_out, keep = refs[:7]
    (
        w_vz_v, w_ab_v, rates_v, gain_v, w_out_v, mig_s, begin, tok_v, post_v,
        kq, ks, qs, q_all, v_all, z_all, d_all, b_all, m_all, h_all, dest, filled, sems,
    ) = refs[7:]
    rows = states.shape[0]
    dim = states.shape[1]
    total = rows * STEPS
    width = w_own_v.shape[0]
    copies = fetch(
        sems, (w_vz, w_vz_v),
        (w_ab, w_ab_v), (rates, rates_v), (mig, mig_s), (states, begin),
        (head_gain, gain_v), (w_out, w_out_v), (tok, tok_v), (post_gain, post_v),
        (moved, keep),
    )
    pieces = (p0, p1, p2, p3, p4, p5, p6, p7)
    x = jnp.concatenate([piece[:, :width] for piece in pieces], axis=0)
    extra = jnp.concatenate([piece[:, width:] for piece in pieces], axis=0).astype(F32)
    live = extra[:, EXTRA - 1 :]
    second = jnp.dot(x, w_other_v[...], preferred_element_type=F32)
    first = jnp.dot(x, w_own_v[...], preferred_element_type=F32)
    copies[3].wait()
    plan_moved(mig_s, filled, dest, rows, moved.shape[0])
    copies[0].wait()
    vz = jnp.dot(x, w_vz_v[...], preferred_element_type=F32)
    for copy in copies[1:3]:
        copy.wait()
    ab = lax.dot_general(
        x, w_ab_v[...], (((1,), (1,)), ((), ())), preferred_element_type=F32
    )
    me = lax.axis_index("expert")
    even = me % 2 == 0
    q = jnp.where(even, first, second)
    k = jnp.where(even, second, first)
    q = q * (lax.rsqrt(jnp.sum(q * q, axis=-1, keepdims=True) + EPS) * dim**-0.5)
    k = k * lax.rsqrt(jnp.sum(k * k, axis=-1, keepdims=True) + EPS)
    beta = jax.nn.sigmoid(ab[:, 1:2])
    rate = jnp.exp(rates_v[0:1, 0:1])
    drive = ab[:, 0:1] + rates_v[1:2, 0:1]
    soft = jnp.maximum(drive, 0.0) + jnp.log1p(jnp.exp(-jnp.abs(drive)))
    decay = jnp.exp(-rate * soft)
    wide = (total, dim)
    q_all[...] = q
    k_out[...] = k
    v_all[...] = vz[:, :dim]
    z_all[...] = vz[:, dim:]
    d_all[...] = jnp.broadcast_to(decay, wide)
    b_all[...] = jnp.broadcast_to(beta, wide)
    m_all[...] = jnp.broadcast_to(live, wide)
    for s in range(rows):
        kq[8 * s : 8 * s + 4] = k[4 * s : 4 * s + 4]
        kq[8 * s + 4 : 8 * s + 8] = q[4 * s : 4 * s + 4]
    for copy in copies[4:]:
        copy.wait()
    place_moved(filled, dest, begin, moved)
    for s in range(rows):
        r = me ^ (2 * (s % (rows // 2)) + s // (rows // 2))
        both = jnp.dot(
            kq[8 * s : 8 * s + 8].astype(BF16), begin[r].astype(BF16), preferred_element_type=F32
        )
        ks[4 * s : 4 * s + 4] = both[:4]
        qs[4 * s : 4 * s + 4] = both[4:]

    def at(ref, t):
        return ref[pl.ds(t, rows, stride=STEPS), :]

    kept = jnp.ones((rows, dim), F32)
    past = []
    gain = gain_v[...]
    for t in range(STEPS):
        k_t, q_t, d_t, m_t = at(k_out, t), at(q_all, t), at(d_all, t), at(m_all, t)
        k_state = kept * at(ks, t)
        q_state = kept * at(qs, t)
        for k_s, w_s in past:
            k_state = k_state + jnp.sum(k_t * k_s, axis=-1, keepdims=True) * w_s
            q_state = q_state + jnp.sum(q_t * k_s, axis=-1, keepdims=True) * w_s
        write = at(b_all, t) * (at(v_all, t) - d_t * k_state)
        o = d_t * q_state + jnp.sum(q_t * k_t, axis=-1, keepdims=True) * write
        scale = lax.rsqrt(jnp.mean(o * o, axis=-1, keepdims=True) + EPS)
        z_t = at(z_all, t)
        h_all[pl.ds(t, rows, stride=STEPS), :] = o * scale * gain * (z_t * jax.nn.sigmoid(z_t))
        alive = m_t > 0.5
        a_t = jnp.where(alive, d_t, 1.0)
        kept = kept * a_t
        past = [(k_s, w_s * a_t) for k_s, w_s in past] + [(k_t, jnp.where(alive, write, 0.0))]
    for t in range(STEPS):
        w_rows[pl.ds(t, rows, stride=STEPS), :] = past[t][1]
    decay_out[...] = kept
    part = jnp.dot(h_all[...].astype(BF16), w_out_v[...], preferred_element_type=F32)
    for u in range(rows // 2):
        chip = (me // 2) ^ u
        own = part[STEPS * u : STEPS * (u + 1)]
        if u == 0:
            own = own + tok_v[...].astype(F32)
        part_own[chip] = own.astype(BF16)
        part_other[chip] = part[STEPS * (rows // 2 + u) : STEPS * (rows // 2 + u + 1)].astype(BF16)
        comb_out[chip, :STEPS] = extra[STEPS * u : STEPS * (u + 1)]
        comb_out[u, STEPS : STEPS + 1] = post_v[:, EXTRA * u : EXTRA * (u + 1)]


def state_kernel(k_in, w_rows, decay, mig, states, *refs):
    moved, out, mig_s, dest, filled, sems = refs
    rows = states.shape[0]
    copies = fetch(
        sems, (mig, mig_s), (states, out)
    )
    for copy in copies:
        copy.wait()
    plan_moved(mig_s, filled, dest, rows, moved.shape[0])
    place_moved(filled, dest, out, moved)
    me = lax.axis_index("expert")
    for s in range(rows):
        r = me ^ (2 * (s % (rows // 2)) + s // (rows // 2))
        k_s = k_in[4 * s : 4 * s + 4, :]
        w_s = w_rows[4 * s : 4 * s + 4, :]
        outer = lax.dot_general(k_s, w_s, (((0,), (0,)), ((), ())), preferred_element_type=F32)
        out[r] = decay[s : s + 1, :] * out[r] + outer


def mixed_kernel(got, out, mixed_out):
    mixed = jnp.sum(got[...].astype(F32), axis=0).astype(BF16)
    mixed_out[...] = mixed
    m = mixed.astype(F32)
    scale = lax.rsqrt(jnp.mean(m * m, axis=-1, keepdims=True) + EPS)
    normed = (m * scale).astype(BF16)
    for j in range(out.shape[0]):
        out[j] = normed


def expert_kernel(
    rows_in, extra_v, up_own_v, up_other_v, down_own_v, down_other_v, out
):
    half = rows_in.shape[0] * STEPS
    me = lax.axis_index("expert")
    partner = me + 1 - 2 * (me % 2)
    extra = extra_v[...]
    gain = jnp.concatenate([extra[j, STEPS : STEPS + 1] for j in range(extra.shape[0])], axis=1)
    x = (rows_in[...].astype(F32).reshape(half, -1) * gain).astype(BF16)
    comb = extra[:, :STEPS].reshape(half, EXTRA)
    lane = lax.broadcasted_iota(jnp.int32, comb.shape, 1)
    total = None
    for index, up, down in ((me, up_own_v, down_own_v), (partner, up_other_v, down_other_v)):
        hidden = down.shape[0]
        proj = jnp.dot(x, up[...], preferred_element_type=F32)
        g, u = proj[:, :hidden], proj[:, hidden:]
        act = (g * jax.nn.sigmoid(g) * u).astype(BF16)
        weight = jnp.sum(jnp.where(lane == index, comb, 0.0), axis=-1, keepdims=True)
        result = weight * jnp.dot(act, down[...], preferred_element_type=F32)
        total = result if total is None else total + result
    total = total.astype(BF16)
    for j in range(out.shape[0]):
        out[j] = total[STEPS * j : STEPS * (j + 1)]


def sum_kernel(got, mixed, out):
    out[...] = (mixed[...].astype(F32) + jnp.sum(got[...].astype(F32), axis=0)).astype(BF16)


def body(
    tokens, route_ids, route_weights, active_mask, migration, state_in, in_gain, query_key,
    value_gate, gates_proj, log_rate, step_bias, head_gain, out_proj, post_gain, expert_up,
    expert_down,
):
    groups = lax.axis_size("dp")
    members = lax.axis_size("expert")
    rows = state_in.shape[0]
    dim = state_in.shape[2]
    width = tokens.shape[2]
    peers = members // 2
    half = rows * STEPS // 2
    total = rows * STEPS
    sds = jax.ShapeDtypeStruct
    vm = pltpu.VMEM
    dma = pltpu.SemaphoreType.DMA
    tok = tokens.reshape(STEPS, width)
    states = state_in.reshape(rows, dim, dim)
    top = route_ids.shape[2]

    w_other = core_swap(query_key)
    payload, parcel = call(
        start_kernel,
        (vm((STEPS, width + EXTRA), BF16), vm((groups, CAP, dim, dim), BF16)),
        [HBM] * 7,
        (VMEM, VMEM),
        scratch=[
            vm((STEPS, width), BF16), vm((1, width), F32), vm((STEPS, top), jnp.int32),
            vm((STEPS, top), BF16), vm((STEPS, rows), jnp.int32),
            vm((groups * rows // 128, 128), jnp.int32), vm((groups * CAP, dim, dim), F32),
            dma((6,)), dma((groups * CAP,)),
        ],
        limit=60,
    )(
        tok, in_gain.reshape(1, width), route_ids.reshape(STEPS, top),
        route_weights.reshape(STEPS, top), active_mask, migration.reshape(-1, 128), states,
    )
    recv = lax.all_to_all(parcel, "dp", split_axis=0, concat_axis=0, tiled=True)
    line = jnp.concatenate([payload] + [hop(payload, m) for m in (2, 4, 6)])
    rates = jnp.broadcast_to(jnp.concatenate([log_rate, step_bias])[:, None], (2, dim))
    pieces = [line] + [hop(line, m) for m in (8, 16, 24)]
    pieces[1], rates = lax.optimization_barrier((pieces[1], rates))
    pieces = pieces + [core_swap(piece) for piece in pieces]

    tall = vm((total, dim), F32)
    plan = [pltpu.SMEM((groups * CAP,), jnp.int32), pltpu.SMEM((groups,), jnp.int32)]
    part_own, part_other, k_rows, w_rows, decay, comb, kept = call(
        heads_kernel,
        (
            sds((peers, STEPS, width), BF16), sds((peers, STEPS, width), BF16),
            sds((total, dim), F32), sds((total, dim), F32), sds((rows, dim), F32),
            sds((peers, 2 * STEPS, EXTRA), F32), sds((groups, CAP, dim, dim), BF16),
        ),
        [VMEM] * 11 + [ANY] + [HBM] * 8,
        (VMEM,) * 6 + (HBM,),
        scratch=[
            vm((width, 2 * dim), BF16), vm((2, width), BF16),
            vm((2, dim), F32),
            vm((1, dim), F32), vm((dim, width), BF16), pltpu.SMEM((groups * rows,), jnp.int32),
            vm((rows, dim, dim), F32), vm((STEPS, width), BF16), vm((1, width), F32),
            vm((2 * total, dim), F32),
        ] + [tall] * 9 + plan + [dma((10,))],
        flops=2 * total * width * 700,
        moved=6 << 20,
        limit=50,
    )(
        *pieces, w_other, recv, query_key, rates, value_gate, gates_proj.T,
        head_gain.reshape(1, dim), out_proj, migration, states, tok, post_gain.reshape(1, width),
    )
    swapped = core_swap(part_other)
    part = (part_own.astype(F32) + swapped.astype(F32)).astype(BF16)
    up_own = expert_up.reshape(width, -1)
    down_own = expert_down.reshape(-1, width)
    hidden = down_own.shape[0]
    part, up_out, down_out = lax.optimization_barrier((part, up_own, down_own))
    up_other = core_swap(up_out)
    down_other = core_swap(down_out)
    got = exchange(part)

    state_out = call(
        state_kernel,
        sds((rows, dim, dim), F32),
        [VMEM] * 3 + [HBM] * 2 + [VMEM],
        VMEM,
        scratch=[pltpu.SMEM((groups * rows,), jnp.int32)] + plan + [dma((2,))],
        flops=2 * total * dim * dim,
        moved=5 << 20,
    )(k_rows, w_rows, decay, migration, states, kept)

    moe, mixed = call(
        mixed_kernel,
        (sds((peers, STEPS, width), BF16), sds((STEPS, width), BF16)),
        [VMEM],
        (VMEM, VMEM),
    )(got)
    moe_rows = exchange(moe)
    served = call(
        expert_kernel,
        vm((peers, STEPS, width), BF16),
        [VMEM] * 6,
        VMEM,
        flops=1 << 29,
        moved=7 << 20,
        limit=10,
    )(moe_rows, comb, up_own, up_other, down_own, down_other)
    back = exchange(served)
    out = call(sum_kernel, sds((STEPS, width), BF16), [VMEM] * 2, VMEM)(back, mixed)
    return (out.reshape(STEPS, 1, width), state_out.reshape(state_in.shape))


def solution(mesh):
    in_specs = (
        P(None, ("dp", "expert"), None),
        P(None, ("dp", "expert"), None),
        P(None, ("dp", "expert"), None),
        P(None, "dp"),
        P(),
        P("dp", "expert", None, None),
        P(),
        P(None, "expert"),
        P(None, "expert"),
        P(None, "expert"),
        P("expert"),
        P("expert"),
        P(),
        P("expert", None),
        P(),
        P("expert", None, None),
        P("expert", None, None),
    )
    out_specs = (P(None, ("dp", "expert"), None), P("dp", "expert", None, None))
    return jax.shard_map(body, mesh=mesh, in_specs=in_specs, out_specs=out_specs, check_vma=False)
```
